512 devices in a mesh: grp: 4 (over y_hi, core), col: 128 (over x, y_lo, z).
Axes of the slice: x: 4, y: 8 (y_hi: 2, y_lo: 4; y = y_hi * 4 + y_lo), z: 8, core: 2. Of those that a mesh axis runs over, the one named last changes fastest.
Arguments:
- spectral: bfloat16 [1280, 128, 1280], P('col', None, 'grp'), may hold values from -0.4375 to 0.4375
- legendre: bfloat16 [1280, 1280, 512], P('col', 'grp'), may hold values from -0.15625 to 0.15625
- wavenumbers: int32 [1280], replicated, may hold values from 0 to 1279, each once
- regime: int32 [512, 88, 1], P(('grp', 'col')), may hold values from 0 to 127; in each aligned block of 88 rows (0 to 87, 88 to 175, ..., all dimensions but the last counted through in order) at most 2 rows name the same one
- daylight: int32 [512, 88], P(('grp', 'col')), may hold values 0 or 1
- gauss_weight: float32 [512], P(('grp', 'col')), may hold values from 106.131996 to 849.05597
- w_in: bfloat16 [128, 64, 512], P('col'), may hold values from -0.75 to 0.75
- b_in: bfloat16 [128, 512], P('col'), may hold values from -3 to 3
- w_out: bfloat16 [128, 16, 512], P('col'), may hold values from -0.25 to 0.25
Outputs:
- heating: bfloat16 [512, 8, 11264], P(('grp', 'col'))
- heating_spectral: bfloat16 [1280, 16, 1280], P('col', None, 'grp')
The draws below stay inside these ranges and needn't reach their ends.
Inputs may be any that keep to these rules, and one draw needn't show every extreme that they name: `wavenumbers`: each wavenumber from 0 to 1279 is held by exactly one slot. Among the 88 blocks of one latitude no regime is named more than 2 times, and in every draw some latitude names some regime exactly 2 times; every regime is named somewhere.
All inputs are finite; a program needn't handle non-finite values. No bound on the sum of `daylight` on one device may be relied on, other than what follows from the above.
Results may differ from the reference program's by a relative error of at most 0.022.
Values may be sent and summed in bfloat16 or wider, within the bound.
No kernel may reach another device: no remote copies, remote signals or barrier semaphores. Data moves between devices by JAX's collectives and lax.ppermute only.
A program may use at most 64 MiB of HBM per device.

```python
import math
import jax
import jax.numpy as jnp
import numpy as np
from jax import lax

LEV = 8
UNITS = 512
NLON = 11264
MTOT = 1280
NDEG = 1280
FEAT = 64
LAT = 512
NBLK = 88
EXPERTS = 128
CAP = 2


def touch_ends(result, stream_key, low, largest):
    longest = result.shape.index(max(result.shape))
    spots = []
    for shift in (0, 1):
        where = [jax.random.randint(jax.random.fold_in(stream_key, axis), (), 0, length) for axis, length in enumerate(result.shape)]
        where[longest] = (where[longest] + shift) % result.shape[longest]
        spots.append(tuple(where))
    return result.at[spots[0]].set(low).at[spots[1]].set(largest)


def levels(rng, shape, cuts, low, high):
    gain = 1.0
    for axis_at, blocks in cuts:
        steps = jax.random.uniform(jax.random.fold_in(jax.random.fold_in(rng, 6), axis_at), (blocks,), jnp.float32, low / len(cuts), high / len(cuts))
        gain = gain * jnp.repeat(jnp.exp(steps), shape[axis_at] // blocks).reshape((-1,) + (1,) * (len(shape) - 1 - axis_at))
    return gain


def deal_out(stream_key, own, number, rows, number_of, top, most, skew):
    order = jax.random.permutation(stream_key, number_of)
    packed, common = shares(number_of, rows * top, most, skew, True), shares(number_of, rows * top, most, skew, False)
    places = jnp.arange(number_of)

    def named(tallies, offset_by):
        used = int((tallies > 0).sum())
        fixed = max(1, used // 4)
        passed = fixed + (places - fixed + offset_by * (used - fixed)) % max(1, number_of - fixed)
        return jnp.zeros((number_of,), jnp.int32).at[order[jnp.where(places < fixed, places, passed)]].set(jnp.asarray(tallies, jnp.int32))

    tallies = jnp.where(number % 4 == 0, named(packed, number // 4), named(common, number - number // 4 - 1))
    mixed = jax.random.permutation(jax.random.fold_in(own, 3), number_of)
    source_of, sink = mixed[0:number_of // 2 * 2:2], mixed[1:number_of // 2 * 2:2]
    margin = jnp.minimum(tallies[source_of] - 1, most - tallies[sink]) // 2
    margin = jnp.where((source_of == order[0]) | (sink == order[0]) | (tallies[sink] == 0), 0, jnp.maximum(margin, 0))
    passed = jax.random.randint(jax.random.fold_in(own, 4), (number_of // 2,), 0, 1 << 20) % (margin + 1)
    tallies = tallies.at[source_of].add(-passed).at[sink].add(passed)
    labels = jnp.searchsorted(jnp.cumsum(tallies), jnp.arange(rows * top), side="right").astype(jnp.int32)
    listing = labels.reshape(top, rows).T
    listing = listing[jax.random.permutation(jax.random.fold_in(own, 1), rows)]
    offset_by = jax.random.randint(jax.random.fold_in(own, 2), (rows, 1), 0, top)
    return jnp.take_along_axis(listing, (jnp.arange(top)[None, :] + offset_by) % top, axis=1)


def shares(count, total, most, skew, full):
    portions = [(1 << 20) // math.isqrt(rank ** skew) + 1 for rank in range(1, count + 1)]
    largest = most if full else min(most, max(-(-total // count), total * portions[0] // sum(portions)))
    least = 1 if total - largest >= count - 1 else 0
    holding, surplus = [largest] + [least] * (count - 1), total - largest - least * (count - 1)
    while surplus > 0:
        movable = [i for i in range(1, count) if holding[i] < largest] or [i for i in range(1, count) if holding[i] < most]
        mass, left = sum([portions[i] for i in movable]), surplus
        for i in movable:
            extra = min(most - holding[i], max(1, left * portions[i] // mass), surplus)
            holding[i] = holding[i] + extra
            surplus = surplus - extra
    return np.array(holding)


def bell_draw(rng, dims, deviation, limit, cuts=(), held_as=jnp.bfloat16):
    array = deviation * jax.random.normal(rng, dims, jnp.float32)
    if cuts:
        array = array * levels(rng, dims, cuts, -0.22, 0.18)
    return jnp.clip(array, -limit, limit).astype(held_as)


def setup_inputs(seed: int = 0) -> dict:
    splits = jax.random.split(jax.random.key(seed), 10)
    spectral = bell_draw(splits[0], (MTOT, 2 * FEAT, NDEG), (MTOT ** -0.5), 0.4375, ((0, 128), (2, 4)))
    legendre = bell_draw(splits[1], (MTOT, NDEG, LAT), NDEG ** -0.5, 0.15625, ((0, 128), (1, 4)))
    wavenumbers = jax.random.permutation(splits[2], MTOT).astype(jnp.int32)
    regime_keys = jax.random.split(jax.random.fold_in(splits[3], 1), LAT * NBLK // NBLK)
    regime_turns = jax.random.permutation(jax.random.fold_in(splits[3], 3), LAT * NBLK // NBLK)
    regime = jax.vmap(lambda own, number: deal_out(jax.random.fold_in(splits[3], 2), own, number, NBLK, EXPERTS, 1, CAP, 2))(regime_keys, regime_turns).reshape((LAT, NBLK, 1))
    daylight = touch_ends((jax.random.randint(splits[4], (LAT, NBLK), 0, 2) < 1).astype(jnp.int32), jax.random.fold_in(splits[4], 1), 0, 1)
    gauss_weight = jnp.clip(jnp.exp(math.log(849.05597) - 2.0794415 * jax.random.uniform(splits[5], (LAT,), jnp.float32) ** levels(splits[5], (LAT,), ((0, 512),), -0.2, 0.2)), 106.131996, 849.05597)
    w_in = bell_draw(splits[6], (EXPERTS, FEAT, UNITS), FEAT ** -0.5, 0.75, ((0, 128),))
    b_in = bell_draw(splits[7], (EXPERTS, UNITS), 0.5, 3.0, ((0, 128),))
    w_out = bell_draw(splits[8], (EXPERTS, 2 * LEV, UNITS), UNITS ** -0.5, 0.25, ((0, 128),))
    return {"spectral": spectral, "legendre": legendre, "wavenumbers": wavenumbers, "regime": regime, "daylight": daylight, "gauss_weight": gauss_weight, "w_in": w_in, "b_in": b_in, "w_out": w_out}


def degree_keep(wavenumbers):
    degree = jnp.arange(NDEG, dtype=jnp.int32)
    return degree[None, :] < (MTOT - wavenumbers)[:, None]


def radiate(blocks, picks, sunlit, w_in, b_in, w_out):
    first = w_in[picks].astype(jnp.float32)
    pre = jnp.einsum('bfh,bfc->bhc', first, blocks.astype(jnp.float32)) + b_in[picks].astype(jnp.float32)[:, :, None]
    act = jax.nn.silu(pre).astype(jnp.bfloat16)
    out = jnp.einsum('boh,bhc->boc', w_out[picks].astype(jnp.float32), act.astype(jnp.float32))
    return (out[:, :LEV] + sunlit.astype(jnp.float32)[:, None, None] * out[:, LEV:]).astype(jnp.bfloat16)


def reference(spectral, legendre, wavenumbers, regime, daylight, gauss_weight, w_in, b_in, w_out):
    keep = degree_keep(wavenumbers)
    masked = jnp.where(keep[:, None, :], spectral, jnp.zeros_like(spectral))

    def inverse(pair):
        table, values = pair
        return jnp.dot(values.astype(jnp.float32), table.astype(jnp.float32), precision=lax.Precision.HIGHEST)

    fourier = lax.map(inverse, (legendre, masked))
    coeffs = jnp.transpose(fourier, (2, 0, 1)).astype(jnp.bfloat16)

    def one_latitude(items):
        coef, picks, sunlit, weight = items
        ordered = jnp.zeros((MTOT, 2 * FEAT), jnp.float32).at[wavenumbers].set(coef.astype(jnp.float32))
        padding = ((0, NLON // 2 + 1 - MTOT), (0, 0))
        real_part = jnp.pad(ordered[:, :FEAT], padding)
        imag_part = jnp.pad(ordered[:, FEAT:], padding)
        values = NLON * jnp.fft.irfft(lax.complex(real_part, imag_part), n=NLON, axis=0)
        columns = jnp.transpose(values).astype(jnp.bfloat16)
        blocks = jnp.transpose(columns.reshape(FEAT, NBLK, 128), (1, 0, 2))
        heat_blocks = radiate(blocks, picks, sunlit, w_in, b_in, w_out)
        heat = jnp.transpose(heat_blocks, (1, 0, 2)).reshape(LEV, NLON)
        spectrum = jnp.fft.rfft(heat.astype(jnp.float32), axis=1)[:, :MTOT] / NLON
        stacked = jnp.concatenate([jnp.transpose(jnp.real(spectrum)), jnp.transpose(jnp.imag(spectrum))], axis=1)
        weighted = (stacked * weight)[wavenumbers].astype(jnp.bfloat16)
        return heat, weighted

    heating, weighted = lax.map(one_latitude, (coeffs, regime[:, :, 0], daylight, gauss_weight))

    def forward(pair):
        table, values = pair
        return jnp.dot(jnp.transpose(values.astype(jnp.float32)), jnp.transpose(table.astype(jnp.float32)), precision=lax.Precision.HIGHEST)

    summed = lax.map(forward, (legendre, jnp.transpose(weighted, (1, 0, 2))))
    heating_spectral = jnp.where(keep[:, None, :], summed, jnp.zeros_like(summed)).astype(jnp.bfloat16)
    return heating, heating_spectral
```

```python
import functools
import math

import jax
import jax.numpy as jnp
import numpy as np
from jax import lax
from jax.sharding import Mesh, PartitionSpec as P
from jax.experimental import pallas as pl
from jax.experimental.pallas import tpu as pltpu

NLON = 11264
BLK = 128
NBLK = NLON // BLK
NHI = 15
BROWS = 96
HALF_ROWS = 176
F32 = jnp.float32
BF16 = jnp.bfloat16


def dot(a, b, ca, cb):
    return lax.dot_general(a, b, (((ca,), (cb,)), ((), ())), preferred_element_type=F32)


def trig(phase, length):
    angle = (np.asarray(phase, np.int64) % length) * (2.0 * np.pi / length)
    return np.cos(angle), np.sin(angle)


def tables():
    c = np.arange(BLK)
    p = np.arange(16)
    cos_pc, sin_pc = trig(np.outer(c, p), BLK)
    live = (p < NHI)[None, :]
    cos_pc, sin_pc = cos_pc * live, sin_pc * live
    first = np.zeros((2, BLK, 16, 2))
    first[0, :, :, 0], first[0, :, :, 1] = cos_pc, -sin_pc
    first[1, :, :, 0], first[1, :, :, 1] = sin_pc, cos_pc
    last = np.zeros((16, 2, 2, BLK))
    last[:, 0, 0], last[:, 0, 1] = cos_pc.T, sin_pc.T
    last[:, 1, 0], last[:, 1, 1] = -sin_pc.T, cos_pc.T
    turn_cos, turn_sin = trig(np.outer(c, c), NLON)
    s = np.arange(BLK)
    cos_sb, sin_sb = trig(np.outer(np.arange(NBLK), s), NBLK)
    cos_sb, sin_sb = cos_sb * (s < NBLK), sin_sb * (s < NBLK)
    second = np.concatenate([2.0 * cos_sb, -2.0 * sin_sb], axis=1)
    inner = np.zeros((2 * BLK, BROWS))
    inner[:BLK, :NBLK], inner[BLK:, :NBLK] = cos_sb.T, -sin_sb.T
    cast = lambda x: jnp.asarray(np.asarray(x, np.float32)).astype(BF16)
    return dict(
        first=cast(first.reshape(2 * BLK, 32)),
        second=cast(second),
        inner=cast(inner),
        last=cast(last.reshape(32, 2 * BLK)),
        turn_cos=jnp.asarray(turn_cos, F32),
        turn_sin=jnp.asarray(turn_sin, F32),
    )


def legendre_kernel(limit_ref, core_ref, table_ref, spec_ref, theirs_ref, ours_ref):
    step = pl.program_id(0)
    width, degrees = spec_ref.shape[1:]
    degree = lax.broadcasted_iota(jnp.int32, (width, degrees), 1)
    spec = spec_ref[0]
    masked = jnp.where(degree < limit_ref[step], spec, jnp.zeros_like(spec))
    core = core_ref[0]
    for which, ref in ((1 - core, theirs_ref), (core, ours_ref)):
        for y_hi in range(2):
            start = pl.multiple_of((2 * y_hi + which) * BLK, BLK)
            part = dot(masked, table_ref[0, :, pl.ds(start, BLK)], 1, 0)
            ref[pl.ds(y_hi * BLK, BLK), :] = part.T.astype(ref.dtype)


def inverse_legendre(spectral, legendre, limit, core):
    slots, width, degrees = spectral.shape
    lats = legendre.shape[2]
    sm = pl.BlockSpec(memory_space=pltpu.SMEM)
    out = pl.BlockSpec((lats // 2, width), lambda s: (0, s))
    return pl.pallas_call(
        legendre_kernel,
        grid=(slots,),
        out_shape=(
            jax.ShapeDtypeStruct((lats // 2, slots * width), BF16),
            jax.ShapeDtypeStruct((lats // 2, slots * width), F32),
        ),
        in_specs=[
            sm,
            sm,
            pl.BlockSpec((1, degrees, lats), lambda s: (s, 0, 0)),
            pl.BlockSpec((1, width, degrees), lambda s: (s, 0, 0)),
        ],
        out_specs=(out, out),
        cost_estimate=pl.CostEstimate(
            flops=2 * slots * width * degrees * lats, bytes_accessed=6_000_000, transcendentals=0
        ),
        name="inverse_legendre",
    )(limit, core, legendre, spectral)


def synth_kernel(coef_ref, pos_ref, first_ref, second_ref, tc_ref, ts_ref, cols_ref, grid_ref, out_ref):
    dests = coef_ref.shape[0] // 2
    local = coef_ref.shape[1] // BLK
    slots = dests * local
    cut = lambda half, i: coef_ref[pl.ds(half * dests, dests), pl.ds(i * BLK, BLK)].astype(F32)
    coef = jnp.concatenate(
        [(cut(0, i) + cut(1, i)).astype(BF16) for i in range(local)], axis=0
    )
    pos = pos_ref[...]
    grid_ref[pl.ds(NHI * BLK, BLK), :] = jnp.zeros((BLK, BLK), F32)

    def place(p, carry):
        want = lax.broadcasted_iota(jnp.int32, (BLK, slots), 0) + p * BLK
        value = jnp.where(want == 0, 0.5, 1.0)
        pick = jnp.where(want == pos, value, 0.0).astype(BF16)
        grid_ref[pl.ds(pl.multiple_of(p * BLK, BLK), BLK), :] = dot(pick, coef, 1, 0).T
        return carry

    lax.fori_loop(0, NHI, place, 0, unroll=3)
    first = first_ref[...]
    second = second_ref[...]
    tc = tc_ref[...]
    ts = ts_ref[...]

    def pair(i, carry):
        f = i * 2
        x = jnp.concatenate(
            [grid_ref[pl.ds(f, 32, stride=64), :], grid_ref[pl.ds(f + 1, 32, stride=64), :]], axis=1
        ).astype(BF16)
        z = dot(first, x, 1, 0)
        rows = []
        for k in range(2):
            re, im = z[:BLK, k * BLK : (k + 1) * BLK], z[BLK:, k * BLK : (k + 1) * BLK]
            rows.append(
                jnp.concatenate([re * tc - im * ts, re * ts + im * tc], axis=1).astype(BF16)
            )
        out = dot(second, jnp.concatenate(rows, axis=0), 1, 1)
        out_ref[pl.ds(f, NBLK, stride=64), :] = out[:, :BLK]
        out_ref[pl.ds(f + 1, NBLK, stride=64), :] = out[:, BLK:]
        return carry

    lax.fori_loop(0, 32, pair, 0, unroll=2)
    cols_ref[...] = out_ref[...].astype(BF16)


def synthesize(coef, pos, tab):
    vm = pl.BlockSpec(memory_space=pltpu.VMEM)
    return pl.pallas_call(
        synth_kernel,
        out_shape=jax.ShapeDtypeStruct((NBLK * 64, BLK), BF16),
        in_specs=[vm] * 6,
        out_specs=vm,
        scratch_shapes=[pltpu.VMEM((16 * BLK, BLK), F32), pltpu.VMEM((NBLK * 64, BLK), F32)],
        compiler_params=pltpu.CompilerParams(vmem_limit_bytes=40 * 1024 * 1024),
        cost_estimate=pl.CostEstimate(flops=3_000_000_000, bytes_accessed=2_500_000, transcendentals=0),
        name="synthesize",
    )(coef, pos, tab["first"], tab["second"], tab["turn_cos"], tab["turn_sin"])


def network_kernel(
    n0, n1, sel_ref, sun_ref, gauss_ref, cols_ref, pos_ref, inner_ref, last_ref, tc_ref, ts_ref, *rest
):
    parts = (rest[:n0], rest[n0 : n0 + n1])
    heat_ref, pay_ref, w_ref, hs_ref, r_ref, sems = rest[n0 + n1 :]

    def fetch(b, carry):
        for half in range(2):
            for d, part in enumerate(parts[half]):

                @pl.when(sel_ref[2 * half, b] == d)
                def _(part=part, half=half):
                    pltpu.make_async_copy(
                        part.at[sel_ref[2 * half + 1, b]], w_ref.at[b, half], sems.at[b, half]
                    ).start()

        return carry

    lax.fori_loop(0, NBLK, fetch, 0)
    hs_ref[...] = jnp.zeros(hs_ref.shape, F32)

    def block(b, carry):
        for half in range(2):
            pltpu.make_async_copy(parts[half][0].at[0], w_ref.at[b, half], sems.at[b, half]).wait()
        cols = cols_ref[pl.ds(pl.multiple_of(b * 64, 64), 64), :]
        out = None
        for half in range(2):
            w = lambda lo, n: w_ref[b, half, pl.ds(lo, n), :]
            w_in = jnp.concatenate([w(0, 64), w(64, 64)], axis=1)
            w_out = jnp.concatenate([w(128, 16), w(144, 16)], axis=1)
            bias = w(160, 16)[:2].astype(F32)
            bias = jnp.concatenate([bias[0:1], bias[1:2]], axis=1)
            pre = dot(cols, w_in, 0, 0) + bias
            h = 0.5 * pre
            act = (h * jnp.tanh(h) + h).astype(BF16)
            part = dot(w_out, act, 1, 1)
            out = part if out is None else out + part
        heat = (out[:8] + sun_ref[b].astype(F32) * out[8:]).astype(BF16)
        heat_ref[:, pl.ds(pl.multiple_of(b * BLK, BLK), BLK)] = heat
        hs_ref[pl.ds(b, 8, stride=BROWS), :] = heat.astype(F32)
        return carry

    lax.fori_loop(0, NBLK, block, 0, unroll=4)
    inner = inner_ref[...]
    last = last_ref[...]
    tc = tc_ref[...]
    ts = ts_ref[...]
    scale = gauss_ref[0] * (1.0 / NLON)
    for lev in range(0, 8, 2):
        h = jnp.concatenate([hs_ref[pl.ds((lev + k) * BROWS, BROWS), :] for k in range(2)], axis=1)
        u = dot(inner, h.astype(BF16), 1, 0)
        rows = []
        for k in range(2):
            re, im = u[:BLK, k * BLK : (k + 1) * BLK], u[BLK:, k * BLK : (k + 1) * BLK]
            rows.append(
                jnp.concatenate([re * tc + im * ts, im * tc - re * ts], axis=1).astype(BF16)
            )
        spec = dot(last, jnp.concatenate(rows, axis=0), 1, 1) * scale
        r_ref[pl.ds(lev, 32, stride=8), :] = spec[:, :BLK]
        r_ref[pl.ds(lev + 1, 32, stride=8), :] = spec[:, BLK:]
    spectrum = jnp.concatenate(
        [r_ref[pl.ds(p * 16, 16), :].astype(BF16) for p in range(NHI)], axis=1
    )
    want = lax.broadcasted_iota(jnp.int32, (NHI * BLK, BLK), 0)
    rows = []
    for i in range(pos_ref.shape[0]):
        pick = jnp.where(want == pos_ref[pl.ds(i, 1), :], 1.0, 0.0).astype(BF16)
        rows.append(dot(spectrum, pick, 1, 0))
    rows.append(jnp.zeros((pay_ref.shape[1] - 16 * len(rows), BLK), F32))
    pay_ref[...] = jnp.concatenate(rows, axis=0).T.astype(BF16)


def network(cols, sel, sun, gauss, pos_local, parts, tab):
    vm = pl.BlockSpec(memory_space=pltpu.VMEM)
    sm = pl.BlockSpec(memory_space=pltpu.SMEM)
    hbm = pl.BlockSpec(memory_space=pl.ANY)
    n0, n1 = len(parts[0]), len(parts[1])
    local, dests = pos_local.shape
    return pl.pallas_call(
        functools.partial(network_kernel, n0, n1),
        out_shape=(
            jax.ShapeDtypeStruct((8, NLON), BF16),
            jax.ShapeDtypeStruct((dests, 2 * BLK), BF16),
        ),
        in_specs=[sm] * 3 + [vm] * 6 + [hbm] * (n0 + n1),
        out_specs=(vm, vm),
        scratch_shapes=[
            pltpu.VMEM((NBLK, 2, HALF_ROWS, BLK), BF16),
            pltpu.VMEM((8 * BROWS, BLK), F32),
            pltpu.VMEM((32 * 8, BLK), F32),
            pltpu.SemaphoreType.DMA((NBLK, 2)),
        ],
        compiler_params=pltpu.CompilerParams(vmem_limit_bytes=48 * 1024 * 1024),
        cost_estimate=pl.CostEstimate(
            flops=4_000_000_000, bytes_accessed=11_000_000, transcendentals=5_800_000
        ),
        name="network",
    )(sel, sun, gauss, cols, pos_local, tab["inner"], tab["last"], tab["turn_cos"], tab["turn_sin"], *parts[0], *parts[1])


AXES = ("y_hi", "core", "x", "y_lo", "z")
SIZES = (2, 2, 4, 4, 8)


def shifted(moves):
    ids = np.arange(math.prod(SIZES)).reshape(SIZES)
    pairs = []
    for (y_hi, core, x, y_lo, z), source in np.ndenumerate(ids):
        axis, by = moves[core]
        y = y_hi * SIZES[3] + y_lo
        if axis == "x":
            x = (x + by) % SIZES[2]
        else:
            y = (y + by) % (SIZES[0] * SIZES[3])
        pairs.append((int(source), int(ids[y // SIZES[3], core, x, y % SIZES[3], z])))
    return pairs


def lines(axes):
    ids = np.arange(math.prod(SIZES)).reshape(SIZES)
    groups = []
    for core in range(2):
        along = 1 if axes[core] == "x" else 2
        groups += np.moveaxis(ids[:, core], along, -1).reshape(-1, 4).tolist()
    return groups


def hop(value, *moves):
    return lax.ppermute(value, AXES, shifted(moves))


def swap(value):
    return lax.ppermute(value, "core", [(0, 1), (1, 0)])


def pack_weights(w_in, b_in, w_out, core):
    lo = core * 256
    parts = []
    cut = lambda a, k: lax.dynamic_slice_in_dim(a, lo + k * BLK, BLK, axis=1)
    parts = [cut(w_in, 0), cut(w_in, 1), cut(w_out, 0), cut(w_out, 1), cut(b_in, 0), cut(b_in, 1)]
    parts.append(jnp.zeros((HALF_ROWS - 162, BLK), BF16))
    return jnp.concatenate(parts, axis=0)


def gather_planes(mine):
    line = lax.all_gather(mine[None], AXES, axis_index_groups=lines(("y", "x")), tiled=True)
    return lax.all_gather(line[None], "z", tiled=True).reshape((32,) + mine.shape)


def gather_rest(plane):
    ahead = hop(plane, ("x", 1), ("y", 1))
    behind = hop(plane, ("x", -1), ("y", -1))
    far_a = hop(ahead[:16], ("x", 1), ("y", 1))
    far_b = hop(behind[16:], ("x", -1), ("y", -1))
    own = [plane, ahead, behind, far_a, far_b]
    other = [swap(part) for part in own]
    return own, other


def places(target):
    z = target % 8
    y = target // 8 % 4
    x = target // 32

    def order(minor, major, me):
        index = z * 4 + minor
        away = (major - me) % 4
        part = jnp.where(away == 0, 0, jnp.where(away == 3, 1, jnp.where(away == 1, 2, 3)))
        part = jnp.where((away == 2) & (index >= 16), 4, part)
        return part, jnp.where(part == 4, index - 16, index)

    by_x = order(y, x, lax.axis_index("x"))
    by_y = order(x, y, lax.axis_index("y_lo"))
    return by_x, by_y


def body(spectral, legendre, wavenumbers, regime, daylight, gauss_weight, w_in, b_in, w_out):
    slots, width, degrees = spectral.shape
    tab = tables()
    core = lax.axis_index("core")
    band = lax.axis_index("y_hi") * 2 + core
    column = (lax.axis_index("x") * 4 + lax.axis_index("y_lo")) * 8 + lax.axis_index("z")
    wave_count = wavenumbers.shape[0]
    dests = wave_count // slots

    mine = lax.dynamic_slice_in_dim(wavenumbers, column * slots, slots)
    degree = band * degrees + jnp.arange(degrees, dtype=jnp.int32)
    keep = degree[None, :] < (wave_count - mine)[:, None]
    place = wavenumbers // NBLK * BLK + wavenumbers % NBLK

    plane = gather_planes(pack_weights(w_in[0], b_in, w_out[0], core))

    limit = wave_count - mine - band * degrees
    theirs, ours = inverse_legendre(spectral, legendre, limit, core[None].astype(jnp.int32))
    pair = (ours + swap(theirs).astype(F32)).astype(BF16)
    got = lax.all_to_all(
        pair.reshape(2 * dests, 2, slots * width // 2),
        ("y_hi", "x", "y_lo", "z"),
        0,
        0,
        tiled=True,
    ).reshape(2 * dests, slots * width)
    local_place = place.reshape(dests, slots).T
    cols = synthesize(got, local_place.reshape(1, wave_count), tab)

    plane, _ = lax.optimization_barrier((plane, got))
    own, other = gather_rest(plane)
    by_x, by_y = places(regime[0, :, 0])
    first = [jnp.where(core == 0, a, b) for a, b in zip(by_x, by_y)]
    second = [jnp.where(core == 0, b, a) for a, b in zip(by_x, by_y)]
    sel = jnp.stack(first + second).astype(jnp.int32)
    heat, pay = network(
        cols, sel, daylight[0], gauss_weight, local_place, (own, other), tab
    )

    pay = jnp.broadcast_to(pay[None], (4,) + pay.shape).reshape(4 * dests, 2, BLK)
    piece = lax.all_to_all(pay, AXES, 0, 0, tiled=True).reshape(4 * dests, 2 * BLK)
    summed = jnp.einsum(
        "skl,lsc->sck",
        legendre,
        piece[:, : slots * 16].reshape(piece.shape[0], slots, 16),
        preferred_element_type=F32,
    )
    heating_spectral = jnp.where(keep[:, None, :], summed, jnp.zeros_like(summed)).astype(BF16)
    return (heat[None], heating_spectral)


def solution(mesh):
    fine = Mesh(mesh.devices.reshape(SIZES), AXES)
    grp, col = ("y_hi", "core"), ("x", "y_lo", "z")
    both = grp + col
    placed = (
        P(col, None, grp),
        P(col, grp, None),
        P(),
        P(both, None, None),
        P(both, None),
        P(both),
        P(col, None, None),
        P(col, None),
        P(col, None, None),
    )
    return jax.shard_map(
        body,
        mesh=fine,
        in_specs=placed,
        out_specs=(P(both, None, None), P(col, None, grp)),
        check_vma=False,
    )
```

```python
import functools
import math

import jax
import jax.numpy as jnp
import numpy as np
from jax import lax
from jax.sharding import Mesh, PartitionSpec as P
from jax.experimental import pallas as pl
from jax.experimental.pallas import tpu as pltpu

NLON = 11264
BLK = 128
NBLK = NLON // BLK
NHI = 15
BROWS = 96
HALF_ROWS = 176
F32 = jnp.float32
BF16 = jnp.bfloat16


def dot(a, b, ca, cb):
    return lax.dot_general(a, b, (((ca,), (cb,)), ((), ())), preferred_element_type=F32)


def trig(phase, length):
    angle = (np.asarray(phase, np.int64) % length) * (2.0 * np.pi / length)
    return np.cos(angle), np.sin(angle)


TURN, INNER, LAST, FIRST, SECOND, ROWS = 0, 256, 512, 576, 832, 1008


def tables():
    c = np.arange(BLK)
    p = np.arange(16)
    cos_pc, sin_pc = trig(np.outer(c, p), BLK)
    live = (p < NHI)[None, :]
    cos_pc, sin_pc = cos_pc * live, sin_pc * live
    first = np.zeros((2, BLK, 16, 2))
    first[0, :, :, 0], first[0, :, :, 1] = cos_pc, -sin_pc
    first[1, :, :, 0], first[1, :, :, 1] = sin_pc, cos_pc
    last = np.zeros((16, 2, 2, BLK))
    last[:, 0, 0], last[:, 0, 1] = cos_pc.T, sin_pc.T
    last[:, 1, 0], last[:, 1, 1] = -sin_pc.T, cos_pc.T
    turn_cos, turn_sin = trig(np.outer(c, c), NLON)
    cos_sb, sin_sb = trig(np.outer(np.arange(NBLK), c), NBLK)
    cos_sb, sin_sb = cos_sb * (c < NBLK), sin_sb * (c < NBLK)
    out = np.zeros((ROWS, BLK), np.float32)
    out[TURN : TURN + BLK], out[TURN + BLK : INNER] = turn_cos, turn_sin
    out[INNER : INNER + BLK, :NBLK], out[INNER + BLK : LAST, :NBLK] = cos_sb.T, -sin_sb.T
    out[LAST:FIRST] = last.reshape(32, 2, BLK).transpose(1, 0, 2).reshape(64, BLK)
    out[FIRST:SECOND, :32] = first.reshape(2 * BLK, 32)
    out[SECOND : SECOND + NBLK], out[SECOND + NBLK :] = 2.0 * cos_sb, -2.0 * sin_sb
    return jnp.asarray(out)


def pack_kernel(core_ref, w_in_ref, b_in_ref, w_out_ref, out_ref):
    core = core_ref[0]
    rows = [[], [], []]
    for k in range(2):
        lanes = pl.ds(pl.multiple_of((2 * core + k) * BLK, BLK), BLK)
        rows[0].append(w_in_ref[0, :, lanes].astype(F32) * 0.5)
        rows[1].append(w_out_ref[0, :, lanes].astype(F32))
        rows[2].append(b_in_ref[:, lanes].astype(F32) * 0.5)
    rows.append([jnp.zeros((HALF_ROWS - 162, BLK), F32)])
    packed = jnp.concatenate(sum(rows, []), axis=0).astype(BF16)
    for k in range(out_ref.shape[0]):
        out_ref[k] = packed


def pack_weights(w_in, b_in, w_out, core, copies):
    vm = pl.BlockSpec(memory_space=pltpu.VMEM)
    return pl.pallas_call(
        pack_kernel,
        out_shape=jax.ShapeDtypeStruct((copies, HALF_ROWS, BLK), BF16),
        in_specs=[pl.BlockSpec(memory_space=pltpu.SMEM)] + [vm] * 3,
        out_specs=vm,
        name="pack_weights",
    )(core, w_in, b_in, w_out)


def legendre_kernel(limit_ref, core_ref, table_ref, spec_ref, theirs_ref, ours_ref):
    slots, degrees, width = spec_ref.shape
    degree = lax.broadcasted_iota(jnp.int32, (degrees, width), 0)
    core = core_ref[0]

    def slot(i, carry):
        spec = spec_ref[i]
        masked = jnp.where(degree < limit_ref[i], spec, jnp.zeros_like(spec))
        lanes = pl.ds(pl.multiple_of(i * BLK, BLK), BLK)
        for which, ref in ((1 - core, theirs_ref), (core, ours_ref)):
            for k, y_hi in enumerate((0, 1)):
                start = pl.multiple_of((2 * y_hi + which) * BLK, BLK)
                part = dot(table_ref[i, :, pl.ds(start, BLK)], masked, 0, 0)
                ref[pl.ds(k * BLK, BLK), lanes] = part.astype(ref.dtype)
        return carry

    lax.fori_loop(0, slots, slot, 0, unroll=10)


def inverse_legendre(spectral, legendre, limit, core):
    slots, degrees, width = spectral.shape
    lats = legendre.shape[2]
    sm = pl.BlockSpec(memory_space=pltpu.SMEM)
    vm = pl.BlockSpec(memory_space=pltpu.VMEM)
    shape = (lats // 2, slots * width)
    return pl.pallas_call(
        legendre_kernel,
        out_shape=(jax.ShapeDtypeStruct(shape, BF16), jax.ShapeDtypeStruct(shape, F32)),
        in_specs=[sm, sm, vm, vm],
        out_specs=(vm, vm),
        cost_estimate=pl.CostEstimate(
            flops=2 * slots * width * degrees * lats, bytes_accessed=6_000_000, transcendentals=0
        ),
        compiler_params=pltpu.CompilerParams(vmem_limit_bytes=24 * 1024 * 1024),
        name="inverse_legendre",
    )(limit, core, legendre, spectral)


def synth_kernel(coef_ref, pos_ref, held_ref, low_ref, high_ref, grid_ref, out_ref, tab_ref, sem):
    fetch = pltpu.make_async_copy(held_ref, tab_ref, sem)
    fetch.start()
    dests, lanes = coef_ref.shape[0] // 2, coef_ref.shape[1]
    slots = dests * lanes // BLK
    coef = []
    for i in range(0, lanes, BLK):
        parts = [coef_ref[pl.ds(k * dests, dests), pl.ds(i, BLK)].astype(F32) for k in range(2)]
        coef.append((parts[0] + parts[1]).astype(BF16))
    coef = jnp.concatenate(coef, axis=0)
    pos = pos_ref[...]
    grid_ref[pl.ds(NHI * BLK, BLK), :] = jnp.zeros((BLK, BLK), F32)

    def place(p, carry):
        want = lax.broadcasted_iota(jnp.int32, (BLK, slots), 0) + p * BLK
        value = jnp.where(want == 0, 0.5, 1.0)
        pick = jnp.where(want == pos, value, 0.0).astype(BF16)
        grid_ref[pl.ds(pl.multiple_of(p * BLK, BLK), BLK), :] = dot(pick, coef, 1, 0).T
        return carry

    lax.fori_loop(0, NHI, place, 0, unroll=5)
    fetch.wait()
    first = tab_ref[pl.ds(FIRST, 2 * BLK), :][:, :32].astype(BF16)
    second = jnp.concatenate(
        [tab_ref[pl.ds(SECOND, NBLK), :], tab_ref[pl.ds(SECOND + NBLK, NBLK), :]], axis=1
    ).astype(BF16)
    tc = tab_ref[pl.ds(TURN, BLK), :]
    ts = tab_ref[pl.ds(TURN + BLK, BLK), :]

    def pair(i, carry):
        f = i * 2
        x = jnp.concatenate(
            [grid_ref[pl.ds(f, 32, stride=64), :], grid_ref[pl.ds(f + 1, 32, stride=64), :]], axis=1
        ).astype(BF16)
        z = dot(first, x, 1, 0)
        rows = []
        for k in range(2):
            re, im = z[:BLK, k * BLK : (k + 1) * BLK], z[BLK:, k * BLK : (k + 1) * BLK]
            rows.append(
                jnp.concatenate([re * tc - im * ts, re * ts + im * tc], axis=1).astype(BF16)
            )
        out = dot(second, jnp.concatenate(rows, axis=0), 1, 1)
        out_ref[pl.ds(f, NBLK, stride=64), :] = out[:, :BLK]
        out_ref[pl.ds(f + 1, NBLK, stride=64), :] = out[:, BLK:]
        return carry

    lax.fori_loop(0, 32, pair, 0, unroll=8)
    rows = low_ref.shape[0]
    low_ref[...] = out_ref[pl.ds(0, rows), :].astype(BF16)
    high_ref[...] = out_ref[pl.ds(rows, rows), :].astype(BF16)


def synthesize(coef, pos, tab):
    vm = pl.BlockSpec(memory_space=pltpu.VMEM)
    return pl.pallas_call(
        synth_kernel,
        out_shape=(jax.ShapeDtypeStruct((NBLK * 32, BLK), BF16),) * 2,
        in_specs=[vm, vm, pl.BlockSpec(memory_space=pl.ANY)],
        out_specs=(vm, vm),
        scratch_shapes=[
            pltpu.VMEM((16 * BLK, BLK), F32),
            pltpu.VMEM((NBLK * 64, BLK), F32),
            pltpu.VMEM((ROWS, BLK), F32),
            pltpu.SemaphoreType.DMA,
        ],
        compiler_params=pltpu.CompilerParams(vmem_limit_bytes=40 * 1024 * 1024),
        cost_estimate=pl.CostEstimate(flops=3_000_000_000, bytes_accessed=2_500_000, transcendentals=0),
        name="synthesize",
    )(coef, pos, tab)


def regime_blocks(at_ref, list_ref, low_ref, high_ref, w_ref, out_ref):
    core, me = at_ref[0], at_ref[1]

    for b in range(NBLK):
        cols_ref, row = (low_ref, b) if b < NBLK // 2 else (high_ref, b - NBLK // 2)
        regime = list_ref[0, b]
        x, y, z = regime // 32, regime // 8 % 4, regime % 8
        minor = jnp.where(core == 0, y, x)
        away = (jnp.where(core == 0, x, y) - me + 4) % 4
        part = jnp.where(away == 0, 0, jnp.where(away == 3, 1, jnp.where(away == 1, 2, 3)))
        e = part * 32 + minor * 8 + z
        cols = cols_ref[pl.ds(row * 64, 64), :]
        w = lambda lo, n: w_ref[e, pl.ds(lo, n), :]
        w_in = jnp.concatenate([w(0, 64), w(64, 64)], axis=1)
        w_out = jnp.concatenate([w(128, 16), w(144, 16)], axis=1)
        bias = w(160, 16)[:2].astype(F32)
        bias = jnp.concatenate([bias[0:1], bias[1:2]], axis=1)
        h = dot(cols, w_in, 0, 0) + bias
        act = (h * jnp.tanh(h) + h).astype(BF16)
        out = dot(w_out, act, 1, 1)
        out_ref[:, pl.ds(b * BLK, BLK)] = out[:8] + list_ref[1, b].astype(F32) * out[8:]


def first_network_kernel(counts, at_ref, list_ref, low_ref, high_ref, *rest):
    parts = rest[: len(counts)]
    out_ref, w_ref, sems = rest[len(counts) :]
    copies = []
    start = 0
    for k, (part, count) in enumerate(zip(parts, counts)):
        copies.append(pltpu.make_async_copy(part, w_ref.at[pl.ds(start, count)], sems.at[k]))
        copies[-1].start()
        start += count
    for copy in copies:
        copy.wait()
    regime_blocks(at_ref, list_ref, low_ref, high_ref, w_ref, out_ref)


def first_network(at, listed, cols, parts):
    vm = pl.BlockSpec(memory_space=pltpu.VMEM)
    sm = pl.BlockSpec(memory_space=pltpu.SMEM)
    hbm = pl.BlockSpec(memory_space=pl.ANY)
    counts = tuple(part.shape[0] for part in parts)
    return pl.pallas_call(
        functools.partial(first_network_kernel, counts),
        out_shape=(
            jax.ShapeDtypeStruct((8, NLON), F32),
            jax.ShapeDtypeStruct((sum(counts), HALF_ROWS, BLK), BF16),
        ),
        in_specs=[sm, sm, vm, vm] + [hbm] * len(parts),
        out_specs=(vm, vm),
        scratch_shapes=[pltpu.SemaphoreType.DMA((len(parts),))],
        compiler_params=pltpu.CompilerParams(vmem_limit_bytes=32 * 1024 * 1024),
        cost_estimate=pl.CostEstimate(
            flops=2_000_000_000, bytes_accessed=13_000_000, transcendentals=2_900_000
        ),
        name="first_network",
    )(at, listed, *cols, *parts)


def second_network(at, listed, cols, weights):
    vm = pl.BlockSpec(memory_space=pltpu.VMEM)
    sm = pl.BlockSpec(memory_space=pltpu.SMEM)
    return pl.pallas_call(
        regime_blocks,
        out_shape=jax.ShapeDtypeStruct((8, NLON), F32),
        in_specs=[sm, sm, vm, vm, vm],
        out_specs=vm,
        compiler_params=pltpu.CompilerParams(vmem_limit_bytes=32 * 1024 * 1024),
        cost_estimate=pl.CostEstimate(
            flops=2_000_000_000, bytes_accessed=8_000_000, transcendentals=2_900_000
        ),
        name="second_network",
    )(at, listed, *cols, weights)


def analysis_kernel(
    gauss_ref, own_ref, got_ref, pos_ref, held_ref, heat_ref, pay_ref, hs_ref, r_ref, tab_ref, sem
):
    fetch = pltpu.make_async_copy(held_ref, tab_ref, sem)
    fetch.start()
    for b in range(NBLK):
        lanes = pl.ds(b * BLK, BLK)
        heat = (own_ref[:, lanes] + got_ref[:, lanes]).astype(BF16)
        heat_ref[:, lanes] = heat
        hs_ref[pl.ds(b, 8, stride=BROWS), :] = heat.astype(F32)
    for lev in range(8):
        hs_ref[pl.ds(lev * BROWS + NBLK, BROWS - NBLK), :] = jnp.zeros((BROWS - NBLK, BLK), F32)
    fetch.wait()
    inner = tab_ref[pl.ds(INNER, 2 * BLK), :][:, :BROWS].astype(BF16)
    last = jnp.concatenate([tab_ref[pl.ds(LAST, 32), :], tab_ref[pl.ds(LAST + 32, 32), :]], axis=1)
    last = last.astype(BF16)
    tc = tab_ref[pl.ds(TURN, BLK), :]
    ts = tab_ref[pl.ds(TURN + BLK, BLK), :]
    scale = gauss_ref[0] * (1.0 / NLON)
    for lev in range(0, 8, 2):
        h = jnp.concatenate([hs_ref[pl.ds((lev + k) * BROWS, BROWS), :] for k in range(2)], axis=1)
        u = dot(inner, h.astype(BF16), 1, 0)
        rows = []
        for k in range(2):
            re, im = u[:BLK, k * BLK : (k + 1) * BLK], u[BLK:, k * BLK : (k + 1) * BLK]
            rows.append(
                jnp.concatenate([re * tc + im * ts, im * tc - re * ts], axis=1).astype(BF16)
            )
        spec = dot(last, jnp.concatenate(rows, axis=0), 1, 1) * scale
        r_ref[pl.ds(lev, 32, stride=8), :] = spec[:, :BLK]
        r_ref[pl.ds(lev + 1, 32, stride=8), :] = spec[:, BLK:]
    spectrum = jnp.concatenate(
        [r_ref[pl.ds(p * 16, 16), :].astype(BF16) for p in range(NHI)], axis=1
    )
    want = lax.broadcasted_iota(jnp.int32, (NHI * BLK, BLK), 0)
    rows = []
    for i in range(pos_ref.shape[0]):
        pick = jnp.where(want == pos_ref[pl.ds(i, 1), :], 1.0, 0.0).astype(BF16)
        rows.append(dot(spectrum, pick, 1, 0))
    rows.append(jnp.zeros((pay_ref.shape[1] - 16 * len(rows), BLK), F32))
    pay_ref[...] = jnp.concatenate(rows, axis=0).T.astype(BF16)


def analyze(gauss, own, got, pos_local, tab):
    vm = pl.BlockSpec(memory_space=pltpu.VMEM)
    sm = pl.BlockSpec(memory_space=pltpu.SMEM)
    return pl.pallas_call(
        analysis_kernel,
        out_shape=(
            jax.ShapeDtypeStruct((8, NLON), BF16),
            jax.ShapeDtypeStruct((pos_local.shape[1], 2 * BLK), BF16),
        ),
        in_specs=[sm] + [vm] * 3 + [pl.BlockSpec(memory_space=pl.ANY)],
        out_specs=(vm, vm),
        scratch_shapes=[
            pltpu.VMEM((8 * BROWS, BLK), F32),
            pltpu.VMEM((32 * 8, BLK), F32),
            pltpu.VMEM((ROWS, BLK), F32),
            pltpu.SemaphoreType.DMA,
        ],
        compiler_params=pltpu.CompilerParams(vmem_limit_bytes=24 * 1024 * 1024),
        cost_estimate=pl.CostEstimate(flops=1_000_000_000, bytes_accessed=1_500_000, transcendentals=0),
        name="analyze",
    )(gauss, own, got, pos_local, tab)


def forward_kernel(limit_ref, core_ref, table_ref, ours_ref, theirs_ref, out_ref):
    slots, degrees, lats = table_ref.shape
    rows = []
    for y_hi in range(2):
        ours = ours_ref[pl.ds(y_hi * BLK, BLK), :]
        theirs = theirs_ref[pl.ds(y_hi * BLK, BLK), :]
        rows += [jnp.where(core_ref[0] == k, ours, theirs) for k in range(2)]
    values = jnp.concatenate(rows, axis=0)
    flipped = jnp.concatenate([values[:, :BLK].astype(F32).T, values[:, BLK:].astype(F32).T], axis=0).astype(BF16)
    degree = lax.broadcasted_iota(jnp.int32, (16, degrees), 1)
    for i in range(slots):
        total = dot(flipped[i * 16 : i * 16 + 16], table_ref[i], 1, 1)
        out_ref[i] = jnp.where(degree < limit_ref[i], total, 0.0).astype(BF16)


def forward_legendre(legendre, ours, theirs, limit, core):
    slots, degrees, lats = legendre.shape
    sm = pl.BlockSpec(memory_space=pltpu.SMEM)
    vm = pl.BlockSpec(memory_space=pltpu.VMEM)
    return pl.pallas_call(
        forward_kernel,
        out_shape=jax.ShapeDtypeStruct((slots, 16, degrees), BF16),
        in_specs=[sm, sm, vm, vm, vm],
        out_specs=vm,
        cost_estimate=pl.CostEstimate(
            flops=32 * slots * degrees * lats, bytes_accessed=4_000_000, transcendentals=0
        ),
        compiler_params=pltpu.CompilerParams(vmem_limit_bytes=16 * 1024 * 1024),
        name="forward_legendre",
    )(limit, core, legendre, ours, theirs)


AXES = ("y_hi", "core", "x", "y_lo", "z")
SIZES = (2, 2, 4, 4, 8)


def moved(value, step):
    ids = np.arange(math.prod(SIZES)).reshape(SIZES)
    pairs = []
    for (y_hi, core, x, y_lo, z), source in np.ndenumerate(ids):
        y = y_hi * SIZES[3] + y_lo
        if core == 0:
            x = (x + step) % SIZES[2]
        else:
            y = (y + step) % (SIZES[0] * SIZES[3])
        pairs.append((int(source), int(ids[y // SIZES[3], core, x, y % SIZES[3], z])))
    return lax.ppermute(value, AXES, pairs)


def sheets():
    ids = np.arange(math.prod(SIZES)).reshape(SIZES)
    groups = ids[:, 0].reshape(-1, 32).tolist()
    return groups + np.swapaxes(ids[:, 1], 1, 2).reshape(-1, 32).tolist()


def swap(value):
    return lax.ppermute(value, "core", [(0, 1), (1, 0)])


def after(value, other):
    return lax.optimization_barrier((value, other))[0]


def exchange(value, axes):
    return lax.all_to_all(value, axes, 0, 0, tiled=True)


def gather_plane(copies):
    return lax.all_to_all(copies, AXES, 0, 0, axis_index_groups=sheets(), tiled=True)


def from_latitudes(pay):
    rows, lanes = pay.shape
    pay = jnp.broadcast_to(pay[None], (2, rows, lanes)).reshape(2 * rows, 2, lanes // 2)
    ours = exchange(pay, ("y_hi", "x", "y_lo", "z")).reshape(2 * rows, lanes)
    return ours, swap(ours)


def body(spectral, legendre, wavenumbers, regime, daylight, gauss_weight, w_in, b_in, w_out):
    slots, width, degrees = spectral.shape
    tab = tables()
    core = lax.axis_index("core").astype(jnp.int32)
    half = lax.axis_index("y_hi").astype(jnp.int32)
    band = half * 2 + core
    column = (lax.axis_index("x") * 4 + lax.axis_index("y_lo")) * 8 + lax.axis_index("z")
    wave_count = wavenumbers.shape[0]

    mine = lax.dynamic_slice_in_dim(wavenumbers, column * slots, slots)
    limit = wave_count - mine - band * degrees
    copies = pack_weights(w_in, b_in, w_out, core[None], 32)
    copies, legendre = lax.optimization_barrier((copies, legendre))
    plane = gather_plane(copies)
    theirs, ours = inverse_legendre(
        jnp.swapaxes(spectral, 1, 2), legendre, limit, core[None]
    )
    pair = (ours + swap(theirs).astype(F32)).astype(BF16)
    pair = pair.reshape(pair.shape[0], 2, -1)
    listed = jnp.stack([regime[0, :, 0], daylight[0]])
    place = wavenumbers // NBLK * BLK + wavenumbers % NBLK
    place = place.reshape(-1, slots).T
    line = place.reshape(1, wave_count)
    plane, pair, listed, place, line = lax.optimization_barrier((plane, pair, listed, place, line))
    coef = exchange(pair, ("y_hi", "x", "y_lo", "z")).reshape(pair.shape[0], -1)
    one, three, sibling = moved(plane, 1), moved(plane, -1), swap(listed)
    coef, one, three, sibling = lax.optimization_barrier((coef, one, three, sibling))
    two = moved(one, 1)

    cols = synthesize(coef, line, tab)
    theirs = tuple(swap(part) for part in cols)

    me = jnp.where(core == 0, lax.axis_index("x"), lax.axis_index("y_lo"))
    at = jnp.stack([core, me.astype(jnp.int32)])
    own, weights = first_network(at, listed, cols, (plane, one, three, two))
    sib = second_network(at, sibling, theirs, weights)
    heat, pay = analyze(gauss_weight, own, swap(sib), place, tab)
    ours, theirs = from_latitudes(pay)
    return (heat[None], forward_legendre(legendre, ours, theirs, limit, core[None]))


def solution(mesh):
    fine = Mesh(mesh.devices.reshape(SIZES), AXES)
    grp, col = ("y_hi", "core"), ("x", "y_lo", "z")
    both = grp + col
    placed = (
        P(col, None, grp),
        P(col, grp, None),
        P(),
        P(both, None, None),
        P(both, None),
        P(both),
        P(col, None, None),
        P(col, None),
        P(col, None, None),
    )
    return jax.shard_map(
        body,
        mesh=fine,
        in_specs=placed,
        out_specs=(P(both, None, None), P(col, None, grp)),
        check_vma=False,
    )
```

```python
import functools
import math

import jax
import jax.numpy as jnp
import numpy as np
from jax import lax
from jax.sharding import Mesh, PartitionSpec as P
from jax.experimental import pallas as pl
from jax.experimental.pallas import tpu as pltpu

NLON = 11264
BLK = 128
NBLK = NLON // BLK
NHI = 15
BROWS = 96
HALF_ROWS = 176
F32 = jnp.float32
BF16 = jnp.bfloat16


def dot(a, b, ca, cb):
    return lax.dot_general(a, b, (((ca,), (cb,)), ((), ())), preferred_element_type=F32)


def trig(phase, length):
    angle = (np.asarray(phase, np.int64) % length) * (2.0 * np.pi / length)
    return np.cos(angle), np.sin(angle)


TURN, INNER, LAST, FIRST, SECOND, ROWS = 0, 256, 512, 576, 832, 1008


def tables():
    c = np.arange(BLK)
    p = np.arange(16)
    cos_pc, sin_pc = trig(np.outer(c, p), BLK)
    live = (p < NHI)[None, :]
    cos_pc, sin_pc = cos_pc * live, sin_pc * live
    first = np.zeros((2, BLK, 16, 2))
    first[0, :, :, 0], first[0, :, :, 1] = cos_pc, -sin_pc
    first[1, :, :, 0], first[1, :, :, 1] = sin_pc, cos_pc
    last = np.zeros((16, 2, 2, BLK))
    last[:, 0, 0], last[:, 0, 1] = cos_pc.T, sin_pc.T
    last[:, 1, 0], last[:, 1, 1] = -sin_pc.T, cos_pc.T
    turn_cos, turn_sin = trig(np.outer(c, c), NLON)
    cos_sb, sin_sb = trig(np.outer(np.arange(NBLK), c), NBLK)
    cos_sb, sin_sb = cos_sb * (c < NBLK), sin_sb * (c < NBLK)
    out = np.zeros((ROWS, BLK), np.float32)
    out[TURN : TURN + BLK], out[TURN + BLK : INNER] = turn_cos, turn_sin
    out[INNER : INNER + BLK, :NBLK], out[INNER + BLK : LAST, :NBLK] = cos_sb.T, -sin_sb.T
    out[LAST:FIRST] = last.reshape(32, 2, BLK).transpose(1, 0, 2).reshape(64, BLK)
    out[FIRST:SECOND, :32] = first.reshape(2 * BLK, 32)
    out[SECOND : SECOND + NBLK], out[SECOND + NBLK :] = 2.0 * cos_sb, -2.0 * sin_sb
    return jnp.asarray(out)


def pack_kernel(core_ref, w_in_ref, b_in_ref, w_out_ref, out_ref):
    core = core_ref[0]
    rows = [[], [], []]
    for k in range(2):
        lanes = pl.ds(pl.multiple_of((2 * core + k) * BLK, BLK), BLK)
        rows[0].append(w_in_ref[0, :, lanes].astype(F32) * 0.5)
        rows[1].append(w_out_ref[0, :, lanes].astype(F32))
        rows[2].append(b_in_ref[:, lanes].astype(F32) * 0.5)
    rows.append([jnp.zeros((HALF_ROWS - 162, BLK), F32)])
    packed = jnp.concatenate(sum(rows, []), axis=0).astype(BF16)
    for k in range(out_ref.shape[0]):
        out_ref[k] = packed


def pack_weights(w_in, b_in, w_out, core, copies):
    vm = pl.BlockSpec(memory_space=pltpu.VMEM)
    return pl.pallas_call(
        pack_kernel,
        out_shape=jax.ShapeDtypeStruct((copies, HALF_ROWS, BLK), BF16),
        in_specs=[pl.BlockSpec(memory_space=pltpu.SMEM)] + [vm] * 3,
        out_specs=vm,
        name="pack_weights",
    )(core, w_in, b_in, w_out)


def legendre_kernel(limit_ref, at_ref, table_ref, spec_ref, theirs_ref, ours_ref):
    slots, degrees, width = spec_ref.shape
    degree = lax.broadcasted_iota(jnp.int32, (degrees, width), 0)
    core, half = at_ref[0], at_ref[1]

    def slot(i, carry):
        spec = spec_ref[i]
        masked = jnp.where(degree < limit_ref[i], spec, jnp.zeros_like(spec))
        lanes = pl.ds(pl.multiple_of(i * BLK, BLK), BLK)
        for which, ref in ((1 - core, theirs_ref), (core, ours_ref)):
            for k, y_hi in enumerate((1 - half, half)):
                start = pl.multiple_of((2 * y_hi + which) * BLK, BLK)
                part = dot(table_ref[i, :, pl.ds(start, BLK)], masked, 0, 0)
                ref[pl.ds(k * BLK, BLK), lanes] = part.astype(ref.dtype)
        return carry

    lax.fori_loop(0, slots, slot, 0, unroll=10)


def inverse_legendre(spectral, legendre, limit, at):
    slots, degrees, width = spectral.shape
    lats = legendre.shape[2]
    sm = pl.BlockSpec(memory_space=pltpu.SMEM)
    vm = pl.BlockSpec(memory_space=pltpu.VMEM)
    shape = (lats // 2, slots * width)
    return pl.pallas_call(
        legendre_kernel,
        out_shape=(jax.ShapeDtypeStruct(shape, BF16), jax.ShapeDtypeStruct(shape, F32)),
        in_specs=[sm, sm, vm, vm],
        out_specs=(vm, vm),
        cost_estimate=pl.CostEstimate(
            flops=2 * slots * width * degrees * lats, bytes_accessed=6_000_000, transcendentals=0
        ),
        compiler_params=pltpu.CompilerParams(vmem_limit_bytes=12 * 1024 * 1024),
        name="inverse_legendre",
    )(limit, at, legendre, spectral)


def synth_kernel(coef_ref, pos_ref, held_ref, low_ref, high_ref, grid_ref, out_ref, tab_ref, sem):
    fetch = pltpu.make_async_copy(held_ref, tab_ref, sem)
    fetch.start()
    dests, lanes = coef_ref.shape
    slots = dests * lanes // BLK
    coef = jnp.concatenate([coef_ref[:, pl.ds(i, BLK)] for i in range(0, lanes, BLK)], axis=0)
    pos = pos_ref[...]
    grid_ref[pl.ds(NHI * BLK, BLK), :] = jnp.zeros((BLK, BLK), F32)

    def place(p, carry):
        want = lax.broadcasted_iota(jnp.int32, (BLK, slots), 0) + p * BLK
        value = jnp.where(want == 0, 0.5, 1.0)
        pick = jnp.where(want == pos, value, 0.0).astype(BF16)
        grid_ref[pl.ds(pl.multiple_of(p * BLK, BLK), BLK), :] = dot(pick, coef, 1, 0).T
        return carry

    lax.fori_loop(0, NHI, place, 0, unroll=5)
    fetch.wait()
    first = tab_ref[pl.ds(FIRST, 2 * BLK), :][:, :32].astype(BF16)
    second = jnp.concatenate(
        [tab_ref[pl.ds(SECOND, NBLK), :], tab_ref[pl.ds(SECOND + NBLK, NBLK), :]], axis=1
    ).astype(BF16)
    tc = tab_ref[pl.ds(TURN, BLK), :]
    ts = tab_ref[pl.ds(TURN + BLK, BLK), :]

    def pair(i, carry):
        f = i * 2
        x = jnp.concatenate(
            [grid_ref[pl.ds(f, 32, stride=64), :], grid_ref[pl.ds(f + 1, 32, stride=64), :]], axis=1
        ).astype(BF16)
        z = dot(first, x, 1, 0)
        rows = []
        for k in range(2):
            re, im = z[:BLK, k * BLK : (k + 1) * BLK], z[BLK:, k * BLK : (k + 1) * BLK]
            rows.append(
                jnp.concatenate([re * tc - im * ts, re * ts + im * tc], axis=1).astype(BF16)
            )
        out = dot(second, jnp.concatenate(rows, axis=0), 1, 1)
        out_ref[pl.ds(f, NBLK, stride=64), :] = out[:, :BLK]
        out_ref[pl.ds(f + 1, NBLK, stride=64), :] = out[:, BLK:]
        return carry

    lax.fori_loop(0, 32, pair, 0, unroll=8)
    rows = low_ref.shape[0]
    low_ref[...] = out_ref[pl.ds(0, rows), :].astype(BF16)
    high_ref[...] = out_ref[pl.ds(rows, rows), :].astype(BF16)


def synthesize(coef, pos, tab):
    vm = pl.BlockSpec(memory_space=pltpu.VMEM)
    return pl.pallas_call(
        synth_kernel,
        out_shape=(jax.ShapeDtypeStruct((NBLK * 32, BLK), BF16),) * 2,
        in_specs=[vm, vm, pl.BlockSpec(memory_space=pl.ANY)],
        out_specs=(vm, vm),
        scratch_shapes=[
            pltpu.VMEM((16 * BLK, BLK), F32),
            pltpu.VMEM((NBLK * 64, BLK), F32),
            pltpu.VMEM((ROWS, BLK), F32),
            pltpu.SemaphoreType.DMA,
        ],
        compiler_params=pltpu.CompilerParams(vmem_limit_bytes=14 * 1024 * 1024),
        cost_estimate=pl.CostEstimate(flops=3_000_000_000, bytes_accessed=2_500_000, transcendentals=0),
        name="synthesize",
    )(coef, pos, tab)


def regime_blocks(at_ref, list_ref, low_ref, high_ref, w_ref, out_ref):
    core, me = at_ref[0], at_ref[1]

    for b in range(NBLK):
        cols_ref, row = (low_ref, b) if b < NBLK // 2 else (high_ref, b - NBLK // 2)
        regime = list_ref[0, b]
        x, y, z = regime // 32, regime // 8 % 4, regime % 8
        minor = jnp.where(core == 0, y, x)
        away = (jnp.where(core == 0, x, y) - me + 4) % 4
        part = jnp.where(away == 0, 0, jnp.where(away == 3, 1, jnp.where(away == 1, 2, 3)))
        e = part * 32 + minor * 8 + z
        cols = cols_ref[pl.ds(row * 64, 64), :]
        w = lambda lo, n: w_ref[e, pl.ds(lo, n), :]
        w_in = jnp.concatenate([w(0, 64), w(64, 64)], axis=1)
        w_out = jnp.concatenate([w(128, 16), w(144, 16)], axis=1)
        bias = w(160, 16)[:2].astype(F32)
        bias = jnp.concatenate([bias[0:1], bias[1:2]], axis=1)
        h = dot(cols, w_in, 0, 0) + bias
        act = (h * jnp.tanh(h) + h).astype(BF16)
        out = dot(w_out, act, 1, 1)
        out_ref[:, pl.ds(b * BLK, BLK)] = out[:8] + list_ref[1, b].astype(F32) * out[8:]


def first_network_kernel(counts, at_ref, list_ref, low_ref, high_ref, *rest):
    parts = rest[: len(counts)]
    out_ref, w_ref, sems = rest[len(counts) :]
    copies = []
    start = 0
    for k, (part, count) in enumerate(zip(parts, counts)):
        copies.append(pltpu.make_async_copy(part, w_ref.at[pl.ds(start, count)], sems.at[k]))
        copies[-1].start()
        start += count
    for copy in copies:
        copy.wait()
    regime_blocks(at_ref, list_ref, low_ref, high_ref, w_ref, out_ref)


def first_network(at, listed, cols, parts):
    vm = pl.BlockSpec(memory_space=pltpu.VMEM)
    sm = pl.BlockSpec(memory_space=pltpu.SMEM)
    hbm = pl.BlockSpec(memory_space=pl.ANY)
    counts = tuple(part.shape[0] for part in parts)
    return pl.pallas_call(
        functools.partial(first_network_kernel, counts),
        out_shape=(
            jax.ShapeDtypeStruct((8, NLON), F32),
            jax.ShapeDtypeStruct((sum(counts), HALF_ROWS, BLK), BF16),
        ),
        in_specs=[sm, sm, vm, vm] + [hbm] * len(parts),
        out_specs=(vm, vm),
        scratch_shapes=[pltpu.SemaphoreType.DMA((len(parts),))],
        compiler_params=pltpu.CompilerParams(vmem_limit_bytes=14 * 1024 * 1024),
        cost_estimate=pl.CostEstimate(
            flops=2_000_000_000, bytes_accessed=13_000_000, transcendentals=2_900_000
        ),
        name="first_network",
    )(at, listed, *cols, *parts)


def second_network(at, listed, cols, weights):
    vm = pl.BlockSpec(memory_space=pltpu.VMEM)
    sm = pl.BlockSpec(memory_space=pltpu.SMEM)
    return pl.pallas_call(
        regime_blocks,
        out_shape=jax.ShapeDtypeStruct((8, NLON), F32),
        in_specs=[sm, sm, vm, vm, vm],
        out_specs=vm,
        compiler_params=pltpu.CompilerParams(vmem_limit_bytes=10 * 1024 * 1024),
        cost_estimate=pl.CostEstimate(
            flops=2_000_000_000, bytes_accessed=8_000_000, transcendentals=2_900_000
        ),
        name="second_network",
    )(at, listed, *cols, weights)


def analysis_kernel(
    gauss_ref, own_ref, got_ref, pos_ref, held_ref, heat_ref, pay_ref, hs_ref, r_ref, tab_ref, sem
):
    fetch = pltpu.make_async_copy(held_ref, tab_ref, sem)
    fetch.start()
    for b in range(NBLK):
        lanes = pl.ds(b * BLK, BLK)
        heat = (own_ref[:, lanes] + got_ref[:, lanes]).astype(BF16)
        heat_ref[:, lanes] = heat
        hs_ref[pl.ds(b, 8, stride=BROWS), :] = heat.astype(F32)
    for lev in range(8):
        hs_ref[pl.ds(lev * BROWS + NBLK, BROWS - NBLK), :] = jnp.zeros((BROWS - NBLK, BLK), F32)
    fetch.wait()
    inner = tab_ref[pl.ds(INNER, 2 * BLK), :][:, :BROWS].astype(BF16)
    last = jnp.concatenate([tab_ref[pl.ds(LAST, 32), :], tab_ref[pl.ds(LAST + 32, 32), :]], axis=1)
    last = last.astype(BF16)
    tc = tab_ref[pl.ds(TURN, BLK), :]
    ts = tab_ref[pl.ds(TURN + BLK, BLK), :]
    scale = gauss_ref[0] * (1.0 / NLON)
    for lev in range(0, 8, 2):
        h = jnp.concatenate([hs_ref[pl.ds((lev + k) * BROWS, BROWS), :] for k in range(2)], axis=1)
        u = dot(inner, h.astype(BF16), 1, 0)
        rows = []
        for k in range(2):
            re, im = u[:BLK, k * BLK : (k + 1) * BLK], u[BLK:, k * BLK : (k + 1) * BLK]
            rows.append(
                jnp.concatenate([re * tc + im * ts, im * tc - re * ts], axis=1).astype(BF16)
            )
        spec = dot(last, jnp.concatenate(rows, axis=0), 1, 1) * scale
        r_ref[pl.ds(lev, 32, stride=8), :] = spec[:, :BLK]
        r_ref[pl.ds(lev + 1, 32, stride=8), :] = spec[:, BLK:]
    spectrum = jnp.concatenate(
        [r_ref[pl.ds(p * 16, 16), :].astype(BF16) for p in range(NHI)], axis=1
    )
    want = lax.broadcasted_iota(jnp.int32, (NHI * BLK, BLK), 0)
    rows = []
    for i in range(pos_ref.shape[0]):
        pick = jnp.where(want == pos_ref[pl.ds(i, 1), :], 1.0, 0.0).astype(BF16)
        rows.append(dot(spectrum, pick, 1, 0))
    rows.append(jnp.zeros((pay_ref.shape[1] - 16 * len(rows), BLK), F32))
    pay = jnp.concatenate(rows, axis=0).T.astype(BF16)
    for y_hi in range(2):
        pay_ref[pl.ds(y_hi * BLK, BLK), :] = pay


def analyze(gauss, own, got, pos_local, tab):
    vm = pl.BlockSpec(memory_space=pltpu.VMEM)
    sm = pl.BlockSpec(memory_space=pltpu.SMEM)
    return pl.pallas_call(
        analysis_kernel,
        out_shape=(
            jax.ShapeDtypeStruct((8, NLON), BF16),
            jax.ShapeDtypeStruct((2 * pos_local.shape[1], 2 * BLK), BF16),
        ),
        in_specs=[sm] + [vm] * 3 + [pl.BlockSpec(memory_space=pl.ANY)],
        out_specs=(vm, vm),
        scratch_shapes=[
            pltpu.VMEM((8 * BROWS, BLK), F32),
            pltpu.VMEM((32 * 8, BLK), F32),
            pltpu.VMEM((ROWS, BLK), F32),
            pltpu.SemaphoreType.DMA,
        ],
        compiler_params=pltpu.CompilerParams(vmem_limit_bytes=8 * 1024 * 1024),
        cost_estimate=pl.CostEstimate(flops=1_000_000_000, bytes_accessed=1_500_000, transcendentals=0),
        name="analyze",
    )(gauss, own, got, pos_local, tab)


def forward_kernel(limit_ref, core_ref, table_ref, ours_ref, theirs_ref, out_ref):
    slots, degrees, lats = table_ref.shape
    rows = []
    for y_hi in range(2):
        ours = ours_ref[pl.ds(y_hi * BLK, BLK), :]
        theirs = theirs_ref[pl.ds(y_hi * BLK, BLK), :]
        rows += [jnp.where(core_ref[0] == k, ours, theirs) for k in range(2)]
    values = jnp.concatenate(rows, axis=0)
    flipped = jnp.concatenate([values[:, :BLK].astype(F32).T, values[:, BLK:].astype(F32).T], axis=0).astype(BF16)
    degree = lax.broadcasted_iota(jnp.int32, (16, degrees), 1)
    for i in range(slots):
        total = dot(flipped[i * 16 : i * 16 + 16], table_ref[i], 1, 1)
        out_ref[i] = jnp.where(degree < limit_ref[i], total, 0.0).astype(BF16)


def forward_legendre(legendre, ours, theirs, limit, core):
    slots, degrees, lats = legendre.shape
    sm = pl.BlockSpec(memory_space=pltpu.SMEM)
    vm = pl.BlockSpec(memory_space=pltpu.VMEM)
    return pl.pallas_call(
        forward_kernel,
        out_shape=jax.ShapeDtypeStruct((slots, 16, degrees), BF16),
        in_specs=[sm, sm, vm, vm, vm],
        out_specs=vm,
        cost_estimate=pl.CostEstimate(
            flops=32 * slots * degrees * lats, bytes_accessed=4_000_000, transcendentals=0
        ),
        compiler_params=pltpu.CompilerParams(vmem_limit_bytes=8 * 1024 * 1024),
        name="forward_legendre",
    )(limit, core, legendre, ours, theirs)


AXES = ("y_hi", "core", "x", "y_lo", "z")
SIZES = (2, 2, 4, 4, 8)


def moved(value, step):
    ids = np.arange(math.prod(SIZES)).reshape(SIZES)
    pairs = []
    for (y_hi, core, x, y_lo, z), source in np.ndenumerate(ids):
        y = y_hi * SIZES[3] + y_lo
        if core == 0:
            x = (x + step) % SIZES[2]
        else:
            y = (y + step) % (SIZES[0] * SIZES[3])
        pairs.append((int(source), int(ids[y // SIZES[3], core, x, y % SIZES[3], z])))
    return lax.ppermute(value, AXES, pairs)


def sheets():
    ids = np.arange(math.prod(SIZES)).reshape(SIZES)
    groups = ids[:, 0].reshape(-1, 32).tolist()
    return groups + np.swapaxes(ids[:, 1], 1, 2).reshape(-1, 32).tolist()


def swap(value):
    return lax.ppermute(value, "core", [(0, 1), (1, 0)])


def after(value, other):
    return lax.optimization_barrier((value, other))[0]


def exchange(value, axes):
    return lax.all_to_all(value, axes, 0, 0, tiled=True)


def gather_plane(copies):
    return lax.all_to_all(copies, AXES, 0, 0, axis_index_groups=sheets(), tiled=True)


def from_latitudes(pay):
    rows, lanes = pay.shape
    pay = pay.reshape(rows, 2, lanes // 2)
    ours = exchange(pay, ("y_hi", "x", "y_lo", "z")).reshape(rows, lanes)
    return ours, swap(ours)


def body(spectral, legendre, wavenumbers, regime, daylight, gauss_weight, w_in, b_in, w_out):
    slots, width, degrees = spectral.shape
    tab = tables()
    core = lax.axis_index("core").astype(jnp.int32)
    half = lax.axis_index("y_hi").astype(jnp.int32)
    band = half * 2 + core
    column = (lax.axis_index("x") * 4 + lax.axis_index("y_lo")) * 8 + lax.axis_index("z")
    wave_count = wavenumbers.shape[0]

    mine = lax.dynamic_slice_in_dim(wavenumbers, column * slots, slots)
    limit = wave_count - mine - band * degrees
    copies = pack_weights(w_in, b_in, w_out, core[None], 32)
    copies, legendre = lax.optimization_barrier((copies, legendre))
    plane = gather_plane(copies)
    theirs, ours = inverse_legendre(
        jnp.swapaxes(spectral, 1, 2), legendre, limit, jnp.stack([core, half])
    )
    got = swap(theirs)
    rows, lanes = ours.shape[0] // 2, ours.shape[1]
    far = (ours[:rows] + got[:rows].astype(F32)).astype(BF16)
    far = lax.ppermute(far, "y_hi", [(0, 1), (1, 0)])
    near = ours[rows:] + got[rows:].astype(F32) + far.astype(F32)
    near = near.astype(BF16).reshape(rows, 2, lanes // 2)
    listed = jnp.stack([regime[0, :, 0], daylight[0]])
    place = wavenumbers // NBLK * BLK + wavenumbers % NBLK
    place = place.reshape(-1, slots).T
    line = place.reshape(1, wave_count)
    plane, near, listed, place, line = lax.optimization_barrier((plane, near, listed, place, line))
    coef = exchange(near, ("x", "y_lo", "z")).reshape(rows, lanes)
    one, three, sibling = moved(plane, 1), moved(plane, -1), swap(listed)
    coef, sibling = lax.optimization_barrier((coef, sibling))
    two = moved(one, 1)

    cols = synthesize(coef, line, tab)
    theirs = tuple(swap(part) for part in cols)

    me = jnp.where(core == 0, lax.axis_index("x"), lax.axis_index("y_lo"))
    at = jnp.stack([core, me.astype(jnp.int32)])
    sib, weights = first_network(at, sibling, theirs, (plane, one, three, two))
    own = second_network(at, listed, cols, weights)
    heat, pay = analyze(gauss_weight, own, swap(sib), place, tab)
    ours, theirs = from_latitudes(pay)
    return (heat[None], forward_legendre(legendre, ours, theirs, limit, core[None]))


def solution(mesh):
    fine = Mesh(mesh.devices.reshape(SIZES), AXES)
    grp, col = ("y_hi", "core"), ("x", "y_lo", "z")
    both = grp + col
    placed = (
        P(col, None, grp),
        P(col, grp, None),
        P(),
        P(both, None, None),
        P(both, None),
        P(both),
        P(col, None, None),
        P(col, None),
        P(col, None, None),
    )
    return jax.shard_map(
        body,
        mesh=fine,
        in_specs=placed,
        out_specs=(P(both, None, None), P(col, None, grp)),
        check_vma=False,
    )
```

```python
import functools
import math

import jax
import jax.numpy as jnp
import numpy as np
from jax import lax
from jax.sharding import Mesh, PartitionSpec as P
from jax.experimental import pallas as pl
from jax.experimental.pallas import tpu as pltpu

NLON = 11264
BLK = 128
NBLK = NLON // BLK
NHI = 15
BROWS = 96
HALF_ROWS = 176
F32 = jnp.float32
BF16 = jnp.bfloat16


def dot(a, b, ca, cb):
    return lax.dot_general(a, b, (((ca,), (cb,)), ((), ())), preferred_element_type=F32)


def trig(phase, length):
    angle = (np.asarray(phase, np.int64) % length) * (2.0 * np.pi / length)
    return np.cos(angle), np.sin(angle)


TURN, INNER, LAST, FIRST, SECOND, ROWS = 0, 256, 512, 576, 832, 1008


def tables():
    c = np.arange(BLK)
    p = np.arange(16)
    cos_pc, sin_pc = trig(np.outer(c, p), BLK)
    live = (p < NHI)[None, :]
    cos_pc, sin_pc = cos_pc * live, sin_pc * live
    first = np.zeros((2, BLK, 16, 2))
    first[0, :, :, 0], first[0, :, :, 1] = cos_pc, -sin_pc
    first[1, :, :, 0], first[1, :, :, 1] = sin_pc, cos_pc
    last = np.zeros((16, 2, 2, BLK))
    last[:, 0, 0], last[:, 0, 1] = cos_pc.T, sin_pc.T
    last[:, 1, 0], last[:, 1, 1] = -sin_pc.T, cos_pc.T
    turn_cos, turn_sin = trig(np.outer(c, c), NLON)
    cos_sb, sin_sb = trig(np.outer(np.arange(NBLK), c), NBLK)
    cos_sb, sin_sb = cos_sb * (c < NBLK), sin_sb * (c < NBLK)
    out = np.zeros((ROWS, BLK), np.float32)
    out[TURN : TURN + BLK], out[TURN + BLK : INNER] = turn_cos, turn_sin
    out[INNER : INNER + BLK, :NBLK], out[INNER + BLK : LAST, :NBLK] = cos_sb.T, -sin_sb.T
    out[LAST:FIRST] = last.reshape(32, 2, BLK).transpose(1, 0, 2).reshape(64, BLK)
    out[FIRST:SECOND, :32] = first.reshape(2 * BLK, 32)
    out[SECOND : SECOND + NBLK], out[SECOND + NBLK :] = 2.0 * cos_sb, -2.0 * sin_sb
    return jnp.asarray(out)


def pack_kernel(core_ref, w_in_ref, b_in_ref, w_out_ref, out_ref):
    core = core_ref[0]
    rows = [[], [], []]
    for k in range(2):
        lanes = pl.ds(pl.multiple_of((2 * core + k) * BLK, BLK), BLK)
        rows[0].append(w_in_ref[0, :, lanes].astype(F32) * 0.5)
        rows[1].append(w_out_ref[0, :, lanes].astype(F32))
        rows[2].append(b_in_ref[:, lanes].astype(F32) * 0.5)
    rows.append([jnp.zeros((HALF_ROWS - 162, BLK), F32)])
    packed = jnp.concatenate(sum(rows, []), axis=0).astype(BF16)
    for k in range(out_ref.shape[0]):
        out_ref[k] = packed


def pack_weights(w_in, b_in, w_out, core, copies):
    vm = pl.BlockSpec(memory_space=pltpu.VMEM)
    return pl.pallas_call(
        pack_kernel,
        out_shape=jax.ShapeDtypeStruct((copies, HALF_ROWS, BLK), BF16),
        in_specs=[pl.BlockSpec(memory_space=pltpu.SMEM)] + [vm] * 3,
        out_specs=vm,
        name="pack_weights",
    )(core, w_in, b_in, w_out)


def legendre_kernel(limit_ref, at_ref, table_ref, spec_ref, theirs_ref, ours_ref):
    slots, degrees, width = spec_ref.shape
    degree = lax.broadcasted_iota(jnp.int32, (degrees, width), 0)
    core, half = at_ref[0], at_ref[1]

    def slot(i, carry):
        spec = spec_ref[i]
        masked = jnp.where(degree < limit_ref[i], spec, jnp.zeros_like(spec))
        lanes = pl.ds(pl.multiple_of(i * BLK, BLK), BLK)
        for which, ref in ((1 - core, theirs_ref), (core, ours_ref)):
            for k, y_hi in enumerate((1 - half, half)):
                start = pl.multiple_of((2 * y_hi + which) * BLK, BLK)
                part = dot(table_ref[i, :, pl.ds(start, BLK)], masked, 0, 0)
                ref[pl.ds(k * BLK, BLK), lanes] = part.astype(ref.dtype)
        return carry

    lax.fori_loop(0, slots, slot, 0, unroll=10)


def inverse_legendre(spectral, legendre, limit, at):
    slots, degrees, width = spectral.shape
    lats = legendre.shape[2]
    sm = pl.BlockSpec(memory_space=pltpu.SMEM)
    vm = pl.BlockSpec(memory_space=pltpu.VMEM)
    shape = (lats // 2, slots * width)
    return pl.pallas_call(
        legendre_kernel,
        out_shape=(jax.ShapeDtypeStruct(shape, BF16), jax.ShapeDtypeStruct(shape, F32)),
        in_specs=[sm, sm, vm, vm],
        out_specs=(vm, vm),
        cost_estimate=pl.CostEstimate(
            flops=2 * slots * width * degrees * lats, bytes_accessed=6_000_000, transcendentals=0
        ),
        compiler_params=pltpu.CompilerParams(vmem_limit_bytes=12 * 1024 * 1024),
        name="inverse_legendre",
    )(limit, at, legendre, spectral)


def synth_kernel(coef_ref, pos_ref, tab_ref, cols_ref, grid_ref, out_ref):
    dests, lanes = coef_ref.shape
    slots = dests * lanes // BLK
    coef = jnp.concatenate([coef_ref[:, pl.ds(i, BLK)] for i in range(0, lanes, BLK)], axis=0)
    pos = pos_ref[...]
    grid_ref[pl.ds(NHI * BLK, BLK), :] = jnp.zeros((BLK, BLK), F32)

    def place(p, carry):
        want = lax.broadcasted_iota(jnp.int32, (BLK, slots), 0) + p * BLK
        value = jnp.where(want == 0, 0.5, 1.0)
        pick = jnp.where(want == pos, value, 0.0).astype(BF16)
        grid_ref[pl.ds(pl.multiple_of(p * BLK, BLK), BLK), :] = dot(pick, coef, 1, 0).T
        return carry

    lax.fori_loop(0, NHI, place, 0, unroll=5)
    first = tab_ref[pl.ds(FIRST, 2 * BLK), :][:, :32].astype(BF16)
    second = jnp.concatenate(
        [tab_ref[pl.ds(SECOND, NBLK), :], tab_ref[pl.ds(SECOND + NBLK, NBLK), :]], axis=1
    ).astype(BF16)
    tc = tab_ref[pl.ds(TURN, BLK), :]
    ts = tab_ref[pl.ds(TURN + BLK, BLK), :]

    def pair(i, carry):
        f = i * 2
        x = jnp.concatenate(
            [grid_ref[pl.ds(f, 32, stride=64), :], grid_ref[pl.ds(f + 1, 32, stride=64), :]], axis=1
        ).astype(BF16)
        z = dot(first, x, 1, 0)
        rows = []
        for k in range(2):
            re, im = z[:BLK, k * BLK : (k + 1) * BLK], z[BLK:, k * BLK : (k + 1) * BLK]
            rows.append(
                jnp.concatenate([re * tc - im * ts, re * ts + im * tc], axis=1).astype(BF16)
            )
        out = dot(second, jnp.concatenate(rows, axis=0), 1, 1)
        out_ref[pl.ds(f, NBLK, stride=64), :] = out[:, :BLK]
        out_ref[pl.ds(f + 1, NBLK, stride=64), :] = out[:, BLK:]
        return carry

    lax.fori_loop(0, 32, pair, 0, unroll=8)
    cols_ref[...] = out_ref[...].astype(BF16)


def synthesize(coef, pos, tab):
    vm = pl.BlockSpec(memory_space=pltpu.VMEM)
    return pl.pallas_call(
        synth_kernel,
        out_shape=jax.ShapeDtypeStruct((NBLK * 64, BLK), BF16),
        in_specs=[vm] * 3,
        out_specs=vm,
        scratch_shapes=[
            pltpu.VMEM((16 * BLK, BLK), F32),
            pltpu.VMEM((NBLK * 64, BLK), F32),
        ],
        compiler_params=pltpu.CompilerParams(vmem_limit_bytes=14 * 1024 * 1024),
        cost_estimate=pl.CostEstimate(flops=1_000_000_000, bytes_accessed=1_000_000, transcendentals=0),
        name="synthesize",
    )(coef, pos, tab)


def regime_blocks(at_ref, list_ref, cols_ref, w_ref, out_ref):
    core, me = at_ref[0], at_ref[1]

    for b in range(NBLK):
        regime = list_ref[0, b]
        x, y, z = regime // 32, regime // 8 % 4, regime % 8
        minor = jnp.where(core == 0, y, x)
        away = (jnp.where(core == 0, x, y) - me + 4) % 4
        part = jnp.where(away == 0, 0, jnp.where(away == 3, 1, jnp.where(away == 1, 2, 3)))
        e = part * 32 + minor * 8 + z
        cols = cols_ref[pl.ds(b * 64, 64), :]
        w = lambda lo, n: w_ref[e, pl.ds(lo, n), :]
        w_in = jnp.concatenate([w(0, 64), w(64, 64)], axis=1)
        w_out = jnp.concatenate([w(128, 16), w(144, 16)], axis=1)
        bias = w(160, 16)[:2].astype(F32)
        bias = jnp.concatenate([bias[0:1], bias[1:2]], axis=1)
        h = dot(cols, w_in, 0, 0) + bias
        act = (h * jnp.tanh(h) + h).astype(BF16)
        out = dot(w_out, act, 1, 1)
        out_ref[:, pl.ds(b * BLK, BLK)] = out[:8] + list_ref[1, b].astype(F32) * out[8:]


def first_network_kernel(counts, at_ref, list_ref, cols_ref, *rest):
    parts = rest[: len(counts)]
    out_ref, w_ref, sems = rest[len(counts) :]
    copies = []
    start = 0
    for k, (part, count) in enumerate(zip(parts, counts)):
        copies.append(pltpu.make_async_copy(part, w_ref.at[pl.ds(start, count)], sems.at[k]))
        copies[-1].start()
        start += count
    for copy in copies:
        copy.wait()
    regime_blocks(at_ref, list_ref, cols_ref, w_ref, out_ref)


def first_network(at, listed, cols, parts):
    vm = pl.BlockSpec(memory_space=pltpu.VMEM)
    sm = pl.BlockSpec(memory_space=pltpu.SMEM)
    hbm = pl.BlockSpec(memory_space=pl.ANY)
    counts = tuple(part.shape[0] for part in parts)
    return pl.pallas_call(
        functools.partial(first_network_kernel, counts),
        out_shape=(
            jax.ShapeDtypeStruct((8, NLON), F32),
            jax.ShapeDtypeStruct((sum(counts), HALF_ROWS, BLK), BF16),
        ),
        in_specs=[sm, sm, vm] + [hbm] * len(parts),
        out_specs=(vm, vm),
        scratch_shapes=[pltpu.SemaphoreType.DMA((len(parts),))],
        compiler_params=pltpu.CompilerParams(vmem_limit_bytes=14 * 1024 * 1024),
        cost_estimate=pl.CostEstimate(
            flops=2_000_000_000, bytes_accessed=13_000_000, transcendentals=2_900_000
        ),
        name="first_network",
    )(at, listed, cols, *parts)


def second_network(at, listed, cols, weights):
    vm = pl.BlockSpec(memory_space=pltpu.VMEM)
    sm = pl.BlockSpec(memory_space=pltpu.SMEM)
    return pl.pallas_call(
        regime_blocks,
        out_shape=jax.ShapeDtypeStruct((8, NLON), F32),
        in_specs=[sm, sm, vm, vm],
        out_specs=vm,
        compiler_params=pltpu.CompilerParams(vmem_limit_bytes=10 * 1024 * 1024),
        cost_estimate=pl.CostEstimate(
            flops=2_000_000_000, bytes_accessed=8_000_000, transcendentals=2_900_000
        ),
        name="second_network",
    )(at, listed, cols, weights)


def analysis_kernel(
    gauss_ref, own_ref, got_ref, pos_ref, tab_ref, heat_ref, pay_ref, hs_ref, r_ref
):
    for b in range(NBLK):
        lanes = pl.ds(b * BLK, BLK)
        heat = (own_ref[:, lanes] + got_ref[:, lanes]).astype(BF16)
        heat_ref[:, lanes] = heat
        hs_ref[pl.ds(b, 8, stride=BROWS), :] = heat.astype(F32)
    for lev in range(8):
        hs_ref[pl.ds(lev * BROWS + NBLK, BROWS - NBLK), :] = jnp.zeros((BROWS - NBLK, BLK), F32)
    inner = tab_ref[pl.ds(INNER, 2 * BLK), :][:, :BROWS].astype(BF16)
    last = jnp.concatenate([tab_ref[pl.ds(LAST, 32), :], tab_ref[pl.ds(LAST + 32, 32), :]], axis=1)
    last = last.astype(BF16)
    tc = tab_ref[pl.ds(TURN, BLK), :]
    ts = tab_ref[pl.ds(TURN + BLK, BLK), :]
    scale = gauss_ref[0] * (1.0 / NLON)
    for lev in range(0, 8, 2):
        h = jnp.concatenate([hs_ref[pl.ds((lev + k) * BROWS, BROWS), :] for k in range(2)], axis=1)
        u = dot(inner, h.astype(BF16), 1, 0)
        rows = []
        for k in range(2):
            re, im = u[:BLK, k * BLK : (k + 1) * BLK], u[BLK:, k * BLK : (k + 1) * BLK]
            rows.append(
                jnp.concatenate([re * tc + im * ts, im * tc - re * ts], axis=1).astype(BF16)
            )
        spec = dot(last, jnp.concatenate(rows, axis=0), 1, 1) * scale
        r_ref[pl.ds(lev, 32, stride=8), :] = spec[:, :BLK]
        r_ref[pl.ds(lev + 1, 32, stride=8), :] = spec[:, BLK:]
    spectrum = jnp.concatenate(
        [r_ref[pl.ds(p * 16, 16), :].astype(BF16) for p in range(NHI)], axis=1
    )
    want = lax.broadcasted_iota(jnp.int32, (NHI * BLK, BLK), 0)
    rows = []
    for i in range(pos_ref.shape[0]):
        pick = jnp.where(want == pos_ref[pl.ds(i, 1), :], 1.0, 0.0).astype(BF16)
        rows.append(dot(spectrum, pick, 1, 0))
    rows.append(jnp.zeros((pay_ref.shape[1] - 16 * len(rows), BLK), F32))
    pay = jnp.concatenate(rows, axis=0).T.astype(BF16)
    for y_hi in range(2):
        pay_ref[pl.ds(y_hi * BLK, BLK), :] = pay


def analyze(gauss, own, got, pos_local, tab):
    vm = pl.BlockSpec(memory_space=pltpu.VMEM)
    sm = pl.BlockSpec(memory_space=pltpu.SMEM)
    return pl.pallas_call(
        analysis_kernel,
        out_shape=(
            jax.ShapeDtypeStruct((8, NLON), BF16),
            jax.ShapeDtypeStruct((2 * pos_local.shape[1], 2 * BLK), BF16),
        ),
        in_specs=[sm] + [vm] * 4,
        out_specs=(vm, vm),
        scratch_shapes=[
            pltpu.VMEM((8 * BROWS, BLK), F32),
            pltpu.VMEM((32 * 8, BLK), F32),
        ],
        compiler_params=pltpu.CompilerParams(vmem_limit_bytes=8 * 1024 * 1024),
        cost_estimate=pl.CostEstimate(flops=1_000_000_000, bytes_accessed=1_500_000, transcendentals=0),
        name="analyze",
    )(gauss, own, got, pos_local, tab)


def forward_kernel(limit_ref, core_ref, table_ref, ours_ref, theirs_ref, out_ref):
    slots, degrees, lats = table_ref.shape
    rows = []
    for y_hi in range(2):
        ours = ours_ref[pl.ds(y_hi * BLK, BLK), :]
        theirs = theirs_ref[pl.ds(y_hi * BLK, BLK), :]
        rows += [jnp.where(core_ref[0] == k, ours, theirs) for k in range(2)]
    values = jnp.concatenate(rows, axis=0)
    flipped = jnp.concatenate([values[:, :BLK].astype(F32).T, values[:, BLK:].astype(F32).T], axis=0).astype(BF16)
    degree = lax.broadcasted_iota(jnp.int32, (16, degrees), 1)
    for i in range(slots):
        total = dot(flipped[i * 16 : i * 16 + 16], table_ref[i], 1, 1)
        out_ref[i] = jnp.where(degree < limit_ref[i], total, 0.0).astype(BF16)


def forward_legendre(legendre, ours, theirs, limit, core):
    slots, degrees, lats = legendre.shape
    sm = pl.BlockSpec(memory_space=pltpu.SMEM)
    vm = pl.BlockSpec(memory_space=pltpu.VMEM)
    return pl.pallas_call(
        forward_kernel,
        out_shape=jax.ShapeDtypeStruct((slots, 16, degrees), BF16),
        in_specs=[sm, sm, vm, vm, vm],
        out_specs=vm,
        cost_estimate=pl.CostEstimate(
            flops=32 * slots * degrees * lats, bytes_accessed=4_000_000, transcendentals=0
        ),
        compiler_params=pltpu.CompilerParams(vmem_limit_bytes=8 * 1024 * 1024),
        name="forward_legendre",
    )(limit, core, legendre, ours, theirs)


AXES = ("y_hi", "core", "x", "y_lo", "z")
SIZES = (2, 2, 4, 4, 8)


def moved(value, step):
    ids = np.arange(math.prod(SIZES)).reshape(SIZES)
    pairs = []
    for (y_hi, core, x, y_lo, z), source in np.ndenumerate(ids):
        y = y_hi * SIZES[3] + y_lo
        if core == 0:
            x = (x + step) % SIZES[2]
        else:
            y = (y + step) % (SIZES[0] * SIZES[3])
        pairs.append((int(source), int(ids[y // SIZES[3], core, x, y % SIZES[3], z])))
    return lax.ppermute(value, AXES, pairs)


def sheets():
    ids = np.arange(math.prod(SIZES)).reshape(SIZES)
    groups = ids[:, 0].reshape(-1, 32).tolist()
    return groups + np.swapaxes(ids[:, 1], 1, 2).reshape(-1, 32).tolist()


def swap(value):
    return lax.ppermute(value, "core", [(0, 1), (1, 0)])


def after(value, other):
    return lax.optimization_barrier((value, other))[0]


def exchange(value, axes):
    return lax.all_to_all(value, axes, 0, 0, tiled=True)


def gather_plane(copies):
    return lax.all_to_all(copies, AXES, 0, 0, axis_index_groups=sheets(), tiled=True)


def from_latitudes(pay):
    rows, lanes = pay.shape
    pay = pay.reshape(rows, 2, lanes // 2)
    ours = exchange(pay, ("y_hi", "x", "y_lo", "z")).reshape(rows, lanes)
    return ours, swap(ours)


def body(spectral, legendre, wavenumbers, regime, daylight, gauss_weight, w_in, b_in, w_out):
    slots, width, degrees = spectral.shape
    tab = tables()
    core = lax.axis_index("core").astype(jnp.int32)
    half = lax.axis_index("y_hi").astype(jnp.int32)
    band = half * 2 + core
    column = (lax.axis_index("x") * 4 + lax.axis_index("y_lo")) * 8 + lax.axis_index("z")
    wave_count = wavenumbers.shape[0]

    mine = lax.dynamic_slice_in_dim(wavenumbers, column * slots, slots)
    limit = wave_count - mine - band * degrees
    copies = pack_weights(w_in, b_in, w_out, core[None], 32)
    copies, legendre = lax.optimization_barrier((copies, legendre))
    plane = gather_plane(copies)
    theirs, ours = inverse_legendre(
        jnp.swapaxes(spectral, 1, 2), legendre, limit, jnp.stack([core, half])
    )
    got = swap(theirs)
    rows, lanes = ours.shape[0] // 2, ours.shape[1]
    far = (ours[:rows] + got[:rows].astype(F32)).astype(BF16)
    far = lax.ppermute(far, "y_hi", [(0, 1), (1, 0)])
    near = ours[rows:] + got[rows:].astype(F32) + far.astype(F32)
    near = near.astype(BF16)
    near = jnp.stack([near[:, : lanes // 2], near[:, lanes // 2 :]], axis=1)
    listed = jnp.stack([regime[0, :, 0], daylight[0]])
    place = wavenumbers // NBLK * BLK + wavenumbers % NBLK
    place = place.reshape(-1, slots).T
    line = place.reshape(1, wave_count)
    plane, near, listed, place, line = lax.optimization_barrier((plane, near, listed, place, line))
    coef = exchange(near, ("x", "y_lo", "z")).reshape(rows, lanes)
    one, three, sibling = moved(plane, 1), moved(plane, -1), swap(listed)
    coef, sibling = lax.optimization_barrier((coef, sibling))
    two = moved(one, 1)

    cols = synthesize(coef, line, tab)
    theirs = swap(cols)

    me = jnp.where(core == 0, lax.axis_index("x"), lax.axis_index("y_lo"))
    at = jnp.stack([core, me.astype(jnp.int32)])
    own, weights = first_network(at, listed, cols, (plane, one, three, two))
    sib = second_network(at, sibling, theirs, weights)
    heat, pay = analyze(gauss_weight, own, swap(sib), place, tab)
    ours, theirs = from_latitudes(pay)
    return (heat[None], forward_legendre(legendre, ours, theirs, limit, core[None]))


def solution(mesh):
    fine = Mesh(mesh.devices.reshape(SIZES), AXES)
    grp, col = ("y_hi", "core"), ("x", "y_lo", "z")
    both = grp + col
    placed = (
        P(col, None, grp),
        P(col, grp, None),
        P(),
        P(both, None, None),
        P(both, None),
        P(both),
        P(col, None, None),
        P(col, None),
        P(col, None, None),
    )
    return jax.shard_map(
        body,
        mesh=fine,
        in_specs=placed,
        out_specs=(P(both, None, None), P(col, None, grp)),
        check_vma=False,
    )
```

```python
import functools
import math

import jax
import jax.numpy as jnp
import numpy as np
from jax import lax
from jax.sharding import Mesh, PartitionSpec as P
from jax.experimental import pallas as pl
from jax.experimental.pallas import tpu as pltpu

NLON = 11264
BLK = 128
NBLK = NLON // BLK
NHI = 15
BROWS = 96
HALF_ROWS = 176
F32 = jnp.float32
BF16 = jnp.bfloat16


def dot(a, b, ca, cb):
    return lax.dot_general(a, b, (((ca,), (cb,)), ((), ())), preferred_element_type=F32)


def trig(phase, length):
    angle = (np.asarray(phase, np.int64) % length) * (2.0 * np.pi / length)
    return np.cos(angle), np.sin(angle)


TURN, INNER, LAST, FIRST, SECOND, ROWS = 0, 256, 512, 576, 832, 1008


def tables():
    c = np.arange(BLK)
    p = np.arange(16)
    cos_pc, sin_pc = trig(np.outer(c, p), BLK)
    live = (p < NHI)[None, :]
    cos_pc, sin_pc = cos_pc * live, sin_pc * live
    first = np.zeros((2, BLK, 16, 2))
    first[0, :, :, 0], first[0, :, :, 1] = cos_pc, -sin_pc
    first[1, :, :, 0], first[1, :, :, 1] = sin_pc, cos_pc
    last = np.zeros((16, 2, 2, BLK))
    last[:, 0, 0], last[:, 0, 1] = cos_pc.T, sin_pc.T
    last[:, 1, 0], last[:, 1, 1] = -sin_pc.T, cos_pc.T
    turn_cos, turn_sin = trig(np.outer(c, c), NLON)
    cos_sb, sin_sb = trig(np.outer(np.arange(NBLK), c), NBLK)
    cos_sb, sin_sb = cos_sb * (c < NBLK), sin_sb * (c < NBLK)
    out = np.zeros((ROWS, BLK), np.float32)
    out[TURN : TURN + BLK], out[TURN + BLK : INNER] = turn_cos, turn_sin
    out[INNER : INNER + BLK, :NBLK], out[INNER + BLK : LAST, :NBLK] = cos_sb.T, -sin_sb.T
    out[LAST:FIRST] = last.reshape(32, 2, BLK).transpose(1, 0, 2).reshape(64, BLK)
    out[FIRST:SECOND, :32] = first.reshape(2 * BLK, 32)
    out[SECOND : SECOND + NBLK], out[SECOND + NBLK :] = 2.0 * cos_sb, -2.0 * sin_sb
    return jnp.asarray(out)


def pack_kernel(core_ref, w_in_ref, b_in_ref, w_out_ref, out_ref):
    core = core_ref[0]
    rows = [[], [], []]
    for k in range(2):
        lanes = pl.ds(pl.multiple_of((2 * core + k) * BLK, BLK), BLK)
        rows[0].append(w_in_ref[0, :, lanes].astype(F32) * 0.5)
        rows[1].append(w_out_ref[0, :, lanes].astype(F32))
        rows[2].append(b_in_ref[:, lanes].astype(F32) * 0.5)
    rows.append([jnp.zeros((HALF_ROWS - 162, BLK), F32)])
    packed = jnp.concatenate(sum(rows, []), axis=0).astype(BF16)
    for k in range(out_ref.shape[0]):
        out_ref[k] = packed


def pack_weights(w_in, b_in, w_out, core, copies):
    vm = pl.BlockSpec(memory_space=pltpu.VMEM)
    return pl.pallas_call(
        pack_kernel,
        out_shape=jax.ShapeDtypeStruct((copies, HALF_ROWS, BLK), BF16),
        in_specs=[pl.BlockSpec(memory_space=pltpu.SMEM)] + [vm] * 3,
        out_specs=vm,
        name="pack_weights",
    )(core, w_in, b_in, w_out)


def legendre_kernel(limit_ref, at_ref, table_ref, spec_ref, theirs_ref, ours_ref):
    slots, degrees, width = spec_ref.shape
    degree = lax.broadcasted_iota(jnp.int32, (degrees, width), 0)
    core, half = at_ref[0], at_ref[1]

    def slot(i, carry):
        spec = spec_ref[i]
        masked = jnp.where(degree < limit_ref[i], spec, jnp.zeros_like(spec))
        lanes = pl.ds(pl.multiple_of(i * BLK, BLK), BLK)
        for which, ref in ((1 - core, theirs_ref), (core, ours_ref)):
            for k, y_hi in enumerate((1 - half, half)):
                start = pl.multiple_of((2 * y_hi + which) * BLK, BLK)
                part = dot(table_ref[i, :, pl.ds(start, BLK)], masked, 0, 0)
                ref[pl.ds(k * BLK, BLK), lanes] = part.astype(ref.dtype)
        return carry

    lax.fori_loop(0, slots, slot, 0, unroll=10)


def inverse_legendre(spectral, legendre, limit, at):
    slots, degrees, width = spectral.shape
    lats = legendre.shape[2]
    sm = pl.BlockSpec(memory_space=pltpu.SMEM)
    vm = pl.BlockSpec(memory_space=pltpu.VMEM)
    shape = (lats // 2, slots * width)
    return pl.pallas_call(
        legendre_kernel,
        out_shape=(jax.ShapeDtypeStruct(shape, BF16), jax.ShapeDtypeStruct(shape, F32)),
        in_specs=[sm, sm, vm, vm],
        out_specs=(vm, vm),
        cost_estimate=pl.CostEstimate(
            flops=2 * slots * width * degrees * lats, bytes_accessed=6_000_000, transcendentals=0
        ),
        compiler_params=pltpu.CompilerParams(vmem_limit_bytes=12 * 1024 * 1024),
        name="inverse_legendre",
    )(limit, at, legendre, spectral)


def synth_kernel(coef_ref, pos_ref, tab_ref, cols_ref, grid_ref, out_ref):
    dests, lanes = coef_ref.shape
    slots = dests * lanes // BLK
    coef = jnp.concatenate([coef_ref[:, pl.ds(i, BLK)] for i in range(0, lanes, BLK)], axis=0)
    pos = pos_ref[...]
    grid_ref[pl.ds(NHI * BLK, BLK), :] = jnp.zeros((BLK, BLK), F32)

    def place(p, carry):
        want = lax.broadcasted_iota(jnp.int32, (BLK, slots), 0) + p * BLK
        value = jnp.where(want == 0, 0.5, 1.0)
        pick = jnp.where(want == pos, value, 0.0).astype(BF16)
        grid_ref[pl.ds(pl.multiple_of(p * BLK, BLK), BLK), :] = dot(pick, coef, 1, 0).T
        return carry

    lax.fori_loop(0, NHI, place, 0, unroll=5)
    first = tab_ref[pl.ds(FIRST, 2 * BLK), :][:, :32].astype(BF16)
    second = jnp.concatenate(
        [tab_ref[pl.ds(SECOND, NBLK), :], tab_ref[pl.ds(SECOND + NBLK, NBLK), :]], axis=1
    ).astype(BF16)
    tc = tab_ref[pl.ds(TURN, BLK), :]
    ts = tab_ref[pl.ds(TURN + BLK, BLK), :]

    def pair(i, carry):
        f = i * 2
        x = jnp.concatenate(
            [grid_ref[pl.ds(f, 32, stride=64), :], grid_ref[pl.ds(f + 1, 32, stride=64), :]], axis=1
        ).astype(BF16)
        z = dot(first, x, 1, 0)
        rows = []
        for k in range(2):
            re, im = z[:BLK, k * BLK : (k + 1) * BLK], z[BLK:, k * BLK : (k + 1) * BLK]
            rows.append(
                jnp.concatenate([re * tc - im * ts, re * ts + im * tc], axis=1).astype(BF16)
            )
        out = dot(second, jnp.concatenate(rows, axis=0), 1, 1)
        out_ref[pl.ds(f, NBLK, stride=64), :] = out[:, :BLK]
        out_ref[pl.ds(f + 1, NBLK, stride=64), :] = out[:, BLK:]
        return carry

    lax.fori_loop(0, 32, pair, 0, unroll=8)
    cols_ref[...] = out_ref[pl.ds(0, NBLK * 64), :].astype(BF16)


def synthesize(coef, pos, tab):
    vm = pl.BlockSpec(memory_space=pltpu.VMEM)
    return pl.pallas_call(
        synth_kernel,
        out_shape=jax.ShapeDtypeStruct((NBLK * 64, BLK), BF16),
        in_specs=[vm] * 3,
        out_specs=vm,
        scratch_shapes=[
            pltpu.VMEM((17 * BLK, BLK), F32),
            pltpu.VMEM((NBLK * 64 + 64, BLK), F32),
        ],
        compiler_params=pltpu.CompilerParams(vmem_limit_bytes=14 * 1024 * 1024),
        cost_estimate=pl.CostEstimate(flops=1_000_000_000, bytes_accessed=1_000_000, transcendentals=0),
        name="synthesize",
    )(coef, pos, tab)


def regime_blocks(at_ref, list_ref, cols_ref, w_ref, out_ref):
    core, me = at_ref[0], at_ref[1]

    for b in range(NBLK):
        regime = list_ref[0, b]
        x, y, z = regime // 32, regime // 8 % 4, regime % 8
        minor = jnp.where(core == 0, y, x)
        away = (jnp.where(core == 0, x, y) - me + 4) % 4
        part = jnp.where(away == 0, 0, jnp.where(away == 3, 1, jnp.where(away == 1, 2, 3)))
        e = part * 32 + minor * 8 + z
        cols = cols_ref[pl.ds(b * 64, 64), :]
        w = lambda lo, n: w_ref[e, pl.ds(lo, n), :]
        w_in = jnp.concatenate([w(0, 64), w(64, 64)], axis=1)
        w_out = jnp.concatenate([w(128, 16), w(144, 16)], axis=1)
        bias = w(160, 16)[:2].astype(F32)
        bias = jnp.concatenate([bias[0:1], bias[1:2]], axis=1)
        h = dot(cols, w_in, 0, 0) + bias
        act = (h * jnp.tanh(h) + h).astype(BF16)
        out = dot(w_out, act, 1, 1)
        out_ref[:, pl.ds(b * BLK, BLK)] = out[:8] + list_ref[1, b].astype(F32) * out[8:]


def first_network_kernel(counts, at_ref, list_ref, cols_ref, *rest):
    parts = rest[: len(counts)]
    out_ref, w_ref, sems = rest[len(counts) :]
    copies = []
    start = 0
    for k, (part, count) in enumerate(zip(parts, counts)):
        copies.append(pltpu.make_async_copy(part, w_ref.at[pl.ds(start, count)], sems.at[k]))
        copies[-1].start()
        start += count
    for copy in copies:
        copy.wait()
    regime_blocks(at_ref, list_ref, cols_ref, w_ref, out_ref)


def first_network(at, listed, cols, parts):
    vm = pl.BlockSpec(memory_space=pltpu.VMEM)
    sm = pl.BlockSpec(memory_space=pltpu.SMEM)
    hbm = pl.BlockSpec(memory_space=pl.ANY)
    counts = tuple(part.shape[0] for part in parts)
    return pl.pallas_call(
        functools.partial(first_network_kernel, counts),
        out_shape=(
            jax.ShapeDtypeStruct((8, NLON), F32),
            jax.ShapeDtypeStruct((sum(counts), HALF_ROWS, BLK), BF16),
        ),
        in_specs=[sm, sm, vm] + [hbm] * len(parts),
        out_specs=(vm, vm),
        scratch_shapes=[pltpu.SemaphoreType.DMA((len(parts),))],
        compiler_params=pltpu.CompilerParams(vmem_limit_bytes=14 * 1024 * 1024),
        cost_estimate=pl.CostEstimate(
            flops=2_000_000_000, bytes_accessed=13_000_000, transcendentals=2_900_000
        ),
        name="first_network",
    )(at, listed, cols, *parts)


def second_network(at, listed, cols, weights):
    vm = pl.BlockSpec(memory_space=pltpu.VMEM)
    sm = pl.BlockSpec(memory_space=pltpu.SMEM)
    return pl.pallas_call(
        regime_blocks,
        out_shape=jax.ShapeDtypeStruct((8, NLON), F32),
        in_specs=[sm, sm, vm, vm],
        out_specs=vm,
        compiler_params=pltpu.CompilerParams(vmem_limit_bytes=10 * 1024 * 1024),
        cost_estimate=pl.CostEstimate(
            flops=2_000_000_000, bytes_accessed=8_000_000, transcendentals=2_900_000
        ),
        name="second_network",
    )(at, listed, cols, weights)


def analysis_kernel(
    gauss_ref, own_ref, got_ref, pos_ref, tab_ref, heat_ref, pay_ref, hs_ref, r_ref
):
    for b in range(NBLK):
        lanes = pl.ds(b * BLK, BLK)
        heat = (own_ref[:, lanes] + got_ref[:, lanes]).astype(BF16)
        heat_ref[:, lanes] = heat
        hs_ref[pl.ds(b, 8, stride=BROWS), :] = heat.astype(F32)
    for lev in range(8):
        hs_ref[pl.ds(lev * BROWS + NBLK, BROWS - NBLK), :] = jnp.zeros((BROWS - NBLK, BLK), F32)
    inner = tab_ref[pl.ds(INNER, 2 * BLK), :][:, :BROWS].astype(BF16)
    last = jnp.concatenate([tab_ref[pl.ds(LAST, 32), :], tab_ref[pl.ds(LAST + 32, 32), :]], axis=1)
    last = last.astype(BF16)
    tc = tab_ref[pl.ds(TURN, BLK), :]
    ts = tab_ref[pl.ds(TURN + BLK, BLK), :]
    scale = gauss_ref[0] * (1.0 / NLON)
    for lev in range(0, 8, 2):
        h = jnp.concatenate([hs_ref[pl.ds((lev + k) * BROWS, BROWS), :] for k in range(2)], axis=1)
        u = dot(inner, h.astype(BF16), 1, 0)
        rows = []
        for k in range(2):
            re, im = u[:BLK, k * BLK : (k + 1) * BLK], u[BLK:, k * BLK : (k + 1) * BLK]
            rows.append(
                jnp.concatenate([re * tc + im * ts, im * tc - re * ts], axis=1).astype(BF16)
            )
        spec = dot(last, jnp.concatenate(rows, axis=0), 1, 1) * scale
        r_ref[pl.ds(lev, 32, stride=8), :] = spec[:, :BLK]
        r_ref[pl.ds(lev + 1, 32, stride=8), :] = spec[:, BLK:]
    spectrum = jnp.concatenate(
        [r_ref[pl.ds(p * 16, 16), :].astype(BF16) for p in range(NHI)], axis=1
    )
    want = lax.broadcasted_iota(jnp.int32, (NHI * BLK, BLK), 0)
    rows = []
    for i in range(pos_ref.shape[0]):
        pick = jnp.where(want == pos_ref[pl.ds(i, 1), :], 1.0, 0.0).astype(BF16)
        rows.append(dot(spectrum, pick, 1, 0))
    rows.append(jnp.zeros((pay_ref.shape[1] - 16 * len(rows), BLK), F32))
    pay = jnp.concatenate(rows, axis=0).T.astype(BF16)
    for y_hi in range(2):
        pay_ref[pl.ds(y_hi * BLK, BLK), :] = pay


def analyze(gauss, own, got, pos_local, tab):
    vm = pl.BlockSpec(memory_space=pltpu.VMEM)
    sm = pl.BlockSpec(memory_space=pltpu.SMEM)
    return pl.pallas_call(
        analysis_kernel,
        out_shape=(
            jax.ShapeDtypeStruct((8, NLON), BF16),
            jax.ShapeDtypeStruct((2 * pos_local.shape[1], 2 * BLK), BF16),
        ),
        in_specs=[sm] + [vm] * 4,
        out_specs=(vm, vm),
        scratch_shapes=[
            pltpu.VMEM((9 * BROWS, BLK), F32),
            pltpu.VMEM((33 * 8, BLK), F32),
        ],
        compiler_params=pltpu.CompilerParams(vmem_limit_bytes=8 * 1024 * 1024),
        cost_estimate=pl.CostEstimate(flops=1_000_000_000, bytes_accessed=1_500_000, transcendentals=0),
        name="analyze",
    )(gauss, own, got, pos_local, tab)


def forward_kernel(limit_ref, core_ref, table_ref, ours_ref, theirs_ref, out_ref):
    slots, degrees, lats = table_ref.shape
    rows = []
    for y_hi in range(2):
        ours = ours_ref[pl.ds(y_hi * BLK, BLK), :]
        theirs = theirs_ref[pl.ds(y_hi * BLK, BLK), :]
        rows += [jnp.where(core_ref[0] == k, ours, theirs) for k in range(2)]
    values = jnp.concatenate(rows, axis=0)
    flipped = jnp.concatenate([values[:, :BLK].astype(F32).T, values[:, BLK:].astype(F32).T], axis=0).astype(BF16)
    degree = lax.broadcasted_iota(jnp.int32, (16, degrees), 1)
    for i in range(slots):
        total = dot(flipped[i * 16 : i * 16 + 16], table_ref[i], 1, 1)
        out_ref[i] = jnp.where(degree < limit_ref[i], total, 0.0).astype(BF16)


def forward_legendre(legendre, ours, theirs, limit, core):
    slots, degrees, lats = legendre.shape
    sm = pl.BlockSpec(memory_space=pltpu.SMEM)
    vm = pl.BlockSpec(memory_space=pltpu.VMEM)
    return pl.pallas_call(
        forward_kernel,
        out_shape=jax.ShapeDtypeStruct((slots, 16, degrees), BF16),
        in_specs=[sm, sm, vm, vm, vm],
        out_specs=vm,
        cost_estimate=pl.CostEstimate(
            flops=32 * slots * degrees * lats, bytes_accessed=4_000_000, transcendentals=0
        ),
        compiler_params=pltpu.CompilerParams(vmem_limit_bytes=8 * 1024 * 1024),
        name="forward_legendre",
    )(limit, core, legendre, ours, theirs)


AXES = ("y_hi", "core", "x", "y_lo", "z")
SIZES = (2, 2, 4, 4, 8)


def moved(value, step):
    ids = np.arange(math.prod(SIZES)).reshape(SIZES)
    pairs = []
    for (y_hi, core, x, y_lo, z), source in np.ndenumerate(ids):
        y = y_hi * SIZES[3] + y_lo
        if core == 0:
            x = (x + step) % SIZES[2]
        else:
            y = (y + step) % (SIZES[0] * SIZES[3])
        pairs.append((int(source), int(ids[y // SIZES[3], core, x, y % SIZES[3], z])))
    return lax.ppermute(value, AXES, pairs)


def sheets():
    ids = np.arange(math.prod(SIZES)).reshape(SIZES)
    groups = ids[:, 0].reshape(-1, 32).tolist()
    return groups + np.swapaxes(ids[:, 1], 1, 2).reshape(-1, 32).tolist()


def swap(value):
    return lax.ppermute(value, "core", [(0, 1), (1, 0)])


def after(value, other):
    return lax.optimization_barrier((value, other))[0]


def exchange(value, axes):
    return lax.all_to_all(value, axes, 0, 0, tiled=True)


def gather_plane(copies):
    return lax.all_to_all(copies, AXES, 0, 0, axis_index_groups=sheets(), tiled=True)


def from_latitudes(pay):
    rows, lanes = pay.shape
    pay = jnp.stack([pay[:, : lanes // 2], pay[:, lanes // 2 :]], axis=1)
    ours = exchange(pay, ("y_hi", "x", "y_lo", "z")).reshape(rows, lanes)
    return ours, swap(ours)


def body(spectral, legendre, wavenumbers, regime, daylight, gauss_weight, w_in, b_in, w_out):
    slots, width, degrees = spectral.shape
    tab = tables()
    core = lax.axis_index("core").astype(jnp.int32)
    half = lax.axis_index("y_hi").astype(jnp.int32)
    band = half * 2 + core
    column = (lax.axis_index("x") * 4 + lax.axis_index("y_lo")) * 8 + lax.axis_index("z")
    wave_count = wavenumbers.shape[0]

    mine = lax.dynamic_slice_in_dim(wavenumbers, column * slots, slots)
    limit = wave_count - mine - band * degrees
    copies = pack_weights(w_in, b_in, w_out, core[None], 32)
    copies, legendre = lax.optimization_barrier((copies, legendre))
    plane = gather_plane(copies)
    theirs, ours = inverse_legendre(
        jnp.swapaxes(spectral, 1, 2), legendre, limit, jnp.stack([core, half])
    )
    got = swap(theirs)
    rows, lanes = ours.shape[0] // 2, ours.shape[1]
    far = (ours[:rows] + got[:rows].astype(F32)).astype(BF16)
    far = lax.ppermute(far, "y_hi", [(0, 1), (1, 0)])
    near = ours[rows:] + got[rows:].astype(F32) + far.astype(F32)
    near = near.astype(BF16)
    near = jnp.stack([near[:, : lanes // 2], near[:, lanes // 2 :]], axis=1)
    listed = jnp.stack([regime[0, :, 0], daylight[0]])
    place = wavenumbers // NBLK * BLK + wavenumbers % NBLK
    place = place.reshape(-1, slots).T
    line = place.reshape(1, wave_count)
    plane, near, listed, place, line = lax.optimization_barrier((plane, near, listed, place, line))
    coef = exchange(near, ("x", "y_lo", "z")).reshape(rows, lanes)
    one, three, sibling = moved(plane, 1), moved(plane, -1), swap(listed)
    coef, sibling = lax.optimization_barrier((coef, sibling))
    two = moved(one, 1)

    cols = synthesize(coef, line, tab)
    theirs = swap(cols)

    me = jnp.where(core == 0, lax.axis_index("x"), lax.axis_index("y_lo"))
    at = jnp.stack([core, me.astype(jnp.int32)])
    own, weights = first_network(at, listed, cols, (plane, one, three, two))
    sib = second_network(at, sibling, theirs, weights)
    heat, pay = analyze(gauss_weight, own, swap(sib), place, tab)
    ours, theirs = from_latitudes(pay)
    return (heat[None], forward_legendre(legendre, ours, theirs, limit, core[None]))


def solution(mesh):
    fine = Mesh(mesh.devices.reshape(SIZES), AXES)
    grp, col = ("y_hi", "core"), ("x", "y_lo", "z")
    both = grp + col
    placed = (
        P(col, None, grp),
        P(col, grp, None),
        P(),
        P(both, None, None),
        P(both, None),
        P(both),
        P(col, None, None),
        P(col, None),
        P(col, None, None),
    )
    return jax.shard_map(
        body,
        mesh=fine,
        in_specs=placed,
        out_specs=(P(both, None, None), P(col, None, grp)),
        check_vma=False,
    )
```
